512 devices in a mesh: gx: 32 (over x, z_hi, y), gy: 16 (over z_lo, core).
Axes of the slice: x: 4, y: 4, z: 16 (z_hi: 2, z_lo: 8; z = z_hi * 8 + z_lo), core: 2. Of those that a mesh axis runs over, the one named last changes fastest.
Arguments:
- velocity: float32 [3, 256, 256, 128], P(None, 'gx', 'gy'), may hold values from -6 to 6
- viscosity: float32 [256, 256, 128], P('gx', 'gy'), may hold values from 0.5 to 20
- pressure: float32 [256, 256, 128], P('gx', 'gy'), may hold values from -6 to 6
- flags: int32 [256, 256, 128], P('gx', 'gy'), may hold values from 0 to 2
Outputs:
- corrected: float32 [3, 256, 256, 128], P(None, 'gx', 'gy')
The draws below stay inside these ranges and needn't reach their ends.
Inputs may be any that keep to these rules, and one draw needn't show every extreme that they name: `flags`: 0 marks solid, 1 fluid, 2 air.
All inputs are finite; a program needn't handle non-finite values.
Results may differ from the reference program's by a relative error of at most 0.00018.
Values sent between devices are 32-bit elements; how exact they have to be, the bound alone decides.
A program may use at most 64 MiB of HBM per device.

```python
import math
import jax
import jax.numpy as jnp

ITERS = 3
NX = 256
NY = 256
NZ = 128


def with_ends(result, stream_key, low, top_value):
    dims = result.shape
    place = [jax.random.randint(jax.random.fold_in(stream_key, axis), (), 0, dims[axis]) for axis in range(len(dims))]
    result = result.at[tuple(place)].set(low)
    longest = dims.index(max(dims))
    place[longest] = (place[longest] + 1) % dims[longest]
    return result.at[tuple(place)].set(top_value)


def steps_of(rng, dims, split, smallest, top_value):
    loudness, own = 1.0, jax.random.fold_in(rng, 6)
    for position, parts in split:
        heights = jnp.exp(jax.random.uniform(jax.random.fold_in(own, position), (parts,), jnp.float32, smallest / len(split), top_value / len(split)))
        loudness = loudness * jnp.repeat(heights, dims[position] // parts).reshape([-1 if axis == position else 1 for axis in range(len(dims))])
    return loudness


def normal_values(own_key, shape, spread, most, split=(), dtype=jnp.bfloat16):
    values = spread * jax.random.normal(own_key, shape, jnp.float32)
    if split:
        values = values * steps_of(own_key, shape, split, -0.22, 0.18)
    return jnp.clip(values, -most, most).astype(dtype)


def setup_inputs(seed: int = 0) -> dict:
    key_list = jax.random.split(jax.random.key(seed), 5)
    velocity = normal_values(key_list[0], (3, NX, NY, NZ), 1.0, 6.0, ((1, 32), (2, 16)), jnp.float32)
    viscosity = jnp.clip(jnp.exp(math.log(20.0) - 3.6888795 * jax.random.uniform(key_list[1], (NX, NY, NZ), jnp.float32) ** steps_of(key_list[1], (NX, NY, NZ), ((0, 32), (1, 16)), -0.2, 0.2)), 0.5, 20.0)
    pressure = normal_values(key_list[2], (NX, NY, NZ), 1.0, 6.0, ((0, 32), (1, 16)), jnp.float32)
    flags = with_ends(jax.random.randint(key_list[3], (NX, NY, NZ), 0, 3), jax.random.fold_in(key_list[3], 1), 0, 2).astype(jnp.int32)
    return {"velocity": velocity, "viscosity": viscosity, "pressure": pressure, "flags": flags}


def shift_low(array, axis):
    widths = [(0, 0)] * array.ndim
    widths[axis] = (1, 0)
    padded = jnp.pad(array, widths)
    return jax.lax.slice_in_dim(padded, 0, array.shape[axis], axis=axis)

def coefficients(grid_fields):
    visc, press, fluid, opened = (grid_fields[0], grid_fields[1], grid_fields[2], grid_fields[3])
    cell_weight = 2.0 * visc * fluid

    def edge_weight(axis_one, axis_two):
        visc_one = shift_low(visc, axis_one)
        fluid_one = shift_low(fluid, axis_one)
        mean_visc = 0.25 * (visc + visc_one + shift_low(visc, axis_two) + shift_low(visc_one, axis_two))
        most_fluid = jnp.maximum(jnp.maximum(fluid, fluid_one), jnp.maximum(shift_low(fluid, axis_two), shift_low(fluid_one, axis_two)))
        return mean_visc * most_fluid
    weight_xy = edge_weight(0, 1)
    weight_xz = edge_weight(0, 2)
    weight_yz = edge_weight(1, 2)
    inner = (slice(1, -1), slice(1, -1), slice(1, -1))
    active = jnp.stack([(jnp.maximum(fluid, shift_low(fluid, axis)) * opened * shift_low(opened, axis))[inner] for axis in range(3)])
    diag_u = 1.0 + cell_weight[inner] + shift_low(cell_weight, 0)[inner] + weight_xy[inner] + weight_xy[1:-1, 2:, 1:-1] + weight_xz[inner] + weight_xz[1:-1, 1:-1, 2:]
    diag_v = 1.0 + cell_weight[inner] + shift_low(cell_weight, 1)[inner] + weight_xy[inner] + weight_xy[2:, 1:-1, 1:-1] + weight_yz[inner] + weight_yz[1:-1, 1:-1, 2:]
    diag_w = 1.0 + cell_weight[inner] + shift_low(cell_weight, 2)[inner] + weight_xz[inner] + weight_xz[2:, 1:-1, 1:-1] + weight_yz[inner] + weight_yz[1:-1, 2:, 1:-1]
    diagonal = active * jnp.stack([diag_u, diag_v, diag_w]) + (1.0 - active)
    effective = press * fluid
    gradient = jnp.stack([(effective - shift_low(effective, axis))[inner] for axis in range(3)])
    return ((cell_weight, weight_xy, weight_xz, weight_yz), active, diagonal, gradient)

def energy(field, weights):
    cell_weight, weight_xy, weight_xz, weight_yz = weights
    along_u, along_v, along_w = (field[0], field[1], field[2])
    stretch_x = along_u[1:, :-1, :-1] - along_u[:-1, :-1, :-1]
    stretch_y = along_v[:-1, 1:, :-1] - along_v[:-1, :-1, :-1]
    stretch_z = along_w[:-1, :-1, 1:] - along_w[:-1, :-1, :-1]
    total = 0.5 * jnp.sum(cell_weight[:-1, :-1, :-1] * (stretch_x * stretch_x + stretch_y * stretch_y + stretch_z * stretch_z))
    shear_xy = along_u[1:, 1:, :] - along_u[1:, :-1, :] + along_v[1:, 1:, :] - along_v[:-1, 1:, :]
    shear_xz = along_u[1:, :, 1:] - along_u[1:, :, :-1] + along_w[1:, :, 1:] - along_w[:-1, :, 1:]
    shear_yz = along_v[:, 1:, 1:] - along_v[:, 1:, :-1] + along_w[:, 1:, 1:] - along_w[:, :-1, 1:]
    total = total + 0.5 * jnp.sum(weight_xy[1:, 1:, :] * shear_xy * shear_xy)
    total = total + 0.5 * jnp.sum(weight_xz[1:, :, 1:] * shear_xz * shear_xz)
    total = total + 0.5 * jnp.sum(weight_yz[:, 1:, 1:] * shear_yz * shear_yz)
    return total

def apply_padded(field, padded, weights, active):
    forces = jax.grad(energy)(padded, weights)[:, 1:-1, 1:-1, 1:-1]
    return active * (field + forces)

def reference(velocity, viscosity, pressure, flags):
    fluid = (flags == 1).astype(jnp.float32)
    opened = (flags != 0).astype(jnp.float32)
    grid_fields = jnp.pad(jnp.stack([viscosity, pressure, fluid, opened]), ((0, 0), (1, 1), (1, 1), (1, 1)))
    weights, active, diagonal, gradient = coefficients(grid_fields)

    def operate(field):
        return apply_padded(field, jnp.pad(field, ((0, 0), (1, 1), (1, 1), (1, 1))), weights, active)
    started = active * (velocity - gradient)
    corrected = started
    residual = started - operate(started)
    search = residual / diagonal
    norm_now = jnp.sum(residual * search)
    for sweep in range(ITERS):
        image = operate(search)
        step_size = norm_now / jnp.sum(search * image)
        corrected = corrected + step_size * search
        residual = residual - step_size * image
        if sweep + 1 < ITERS:
            scaled = residual / diagonal
            norm_next = jnp.sum(residual * scaled)
            search = scaled + norm_next / norm_now * search
            norm_now = norm_next
    return corrected
```

```python
import jax
import jax.numpy as jnp
from jax import lax
from jax.experimental import pallas as pl
from jax.experimental.pallas import tpu as pltpu
from jax.sharding import PartitionSpec as P

MESH = pl.DeviceIdType.MESH
F32 = jnp.float32
NX, NY, NZ = 8, 16, 128
LOW, HIGH = 4, 3
EX, EY = NX + LOW + HIGH, 24
X0, X1 = LOW, LOW + NX
Y0, Y1 = LOW, LOW + NY
CARD, RING = 32, 16


def low_y(a):
    return pltpu.roll(a, 1, 1)


def next_y(a):
    return pltpu.roll(a, EY - 1, 1)


def lanes(a):
    return lax.broadcasted_iota(jnp.int32, a.shape, a.ndim - 1)


def low_z(a):
    return jnp.where(lanes(a) == 0, 0.0, pltpu.roll(a, 1, a.ndim - 1))


def next_z(a):
    return jnp.where(lanes(a) == NZ - 1, 0.0, pltpu.roll(a, NZ - 1, a.ndim - 1))


def blocks(start, stop, size):
    count = -(-(stop - start) // size)
    edges = [start + (stop - start) * n // count for n in range(count + 1)]
    return list(zip(edges[:-1], edges[1:]))


def kernel(
    gxn, gyn,
    vel, visc, press, flags, out,
    S, V0, V1, V2, VEL, VI, FL, PR, RAW, RAWIN,
    CW, WXY, WXZ, WYZ, EU, EV, DU, DV, DW,
    CARDS, RINGS,
    lsem, xs, xr, ys, yr, cs, cr, rs, rr,
):
    gx, gy = lax.axis_index("gx"), lax.axis_index("gy")
    has_xlo, has_xhi = gx > 0, gx < gxn - 1
    has_ylo, has_yhi = gy > 0, gy < gyn - 1
    xlo, xhi = (gx - 1, gy), (gx + 1, gy)
    ylo, yhi = (gx, gy - 1), (gx, gy + 1)
    px, zh, py = gx // 8, lax.rem(gx // 4, 2), lax.rem(gx, 4)
    zl, core = gy // 2, lax.rem(gy, 2)
    card = (px * 4 + py) * 2 + core
    ring = zh * 8 + zl

    def card_device(r):
        return ((r // 8) * 8 + zh * 4 + lax.rem(r // 2, 4), zl * 2 + lax.rem(r, 2))

    def ring_device(r):
        return (px * 8 + (r // 8) * 4 + py, lax.rem(r, 8) * 2 + core)

    own = (pl.ds(X0, NX), pl.ds(Y0, NY))
    local = [
        pltpu.make_async_copy(flags, FL.at[own], lsem.at[0]),
        pltpu.make_async_copy(press, PR.at[pl.ds(1, NX), pl.ds(Y0, NY)], lsem.at[1]),
        pltpu.make_async_copy(vel, VEL.at[:, :, pl.ds(Y0, NY)], lsem.at[2]),
        pltpu.make_async_copy(visc, VI.at[own], lsem.at[3]),
    ]
    for copy in local:
        copy.start()

    def clear(ref, lead, kind):
        zero = lambda *shape: jnp.zeros(shape, kind)
        for c in range(lead) if lead else [None]:
            at = ref if c is None else ref.at[c]
            at[0:X0] = zero(X0, EY, NZ)
            at[X1:EX] = zero(EX - X1, EY, NZ)
            at[X0:X1, 0:Y0] = zero(NX, Y0, NZ)
            at[X0:X1, Y1:EY] = zero(NX, EY - Y1, NZ)

    clear(S, 3, F32)
    clear(VI, 0, F32)
    clear(FL, 0, jnp.int32)
    PR[0] = jnp.zeros((EY, NZ), F32)
    PR[1:, 0:Y0] = jnp.zeros((NX, Y0, NZ), F32)
    PR[1:, Y1:EY] = jnp.zeros((NX, EY - Y1, NZ), F32)
    RAWIN[...] = jnp.zeros((1, EY, NZ), F32)
    for c in range(3):
        V2[c, X1] = jnp.zeros((EY, NZ), F32)
        VEL[c, :, 0:Y0] = jnp.zeros((NX, Y0, NZ), F32)
        VEL[c, :, Y1:EY] = jnp.zeros((NX, EY - Y1, NZ), F32)

    barrier = pltpu.get_barrier_semaphore()

    def greet(device):
        pl.semaphore_signal(barrier, inc=1, device_id=device, device_id_type=MESH)

    near = [(has_xlo, xlo), (has_xhi, xhi), (has_ylo, ylo), (has_yhi, yhi)]
    for there, device in near:
        pl.when(there)(lambda device=device: greet(device))

    @pl.loop(1, CARD)
    def _(d):
        greet(card_device(lax.rem(card + d, CARD)))

    @pl.loop(1, RING)
    def _(d):
        greet(ring_device(lax.rem(ring + d, RING)))

    one = lambda there: jnp.where(there, 1, 0)
    pl.semaphore_wait(barrier, CARD + RING - 2 + sum(one(t) for t, _ in near))

    sent = []

    def send(source, target, sems, n, to, there, from_):
        copy = pltpu.make_async_remote_copy(
            src_ref=source, dst_ref=target, send_sem=sems[0].at[n], recv_sem=sems[1].at[n],
            device_id=to, device_id_type=MESH,
        )
        pl.when(there)(copy.start)
        sent.append((there, copy))
        return lambda: pl.when(from_)(copy.wait_recv)

    X, Y = (xs, xr), (ys, yr)
    UP, DOWN = (xhi, has_xhi, has_xlo), (xlo, has_xlo, has_xhi)
    NORTH, SOUTH = (yhi, has_yhi, has_ylo), (ylo, has_ylo, has_yhi)
    rows = pl.ds(Y0, NY)
    last4, first3 = pl.ds(NX - LOW, LOW), pl.ds(0, HIGH)
    xlow, xhigh, xown = pl.ds(0, LOW), pl.ds(X1, HIGH), pl.ds(X0, NX)
    ylow, yhigh = pl.ds(0, LOW), pl.ds(Y1, HIGH)
    ylast, yfirst = pl.ds(NY - LOW, LOW), pl.ds(0, HIGH)
    elast, efirst = pl.ds(Y1 - LOW, LOW), pl.ds(Y0, HIGH)

    x_cells = [
        send(flags.at[last4], FL.at[xlow, rows], X, 0, *UP),
        send(flags.at[first3], FL.at[xhigh, rows], X, 1, *DOWN),
        send(visc.at[last4], VI.at[xlow, rows], X, 2, *UP),
        send(visc.at[first3], VI.at[xhigh, rows], X, 3, *DOWN),
    ]
    x_press = send(press.at[pl.ds(NX - 1, 1)], PR.at[pl.ds(0, 1), rows], X, 4, *UP)
    y_press = send(press.at[:, pl.ds(NY - 1, 1)], PR.at[pl.ds(1, NX), pl.ds(Y0 - 1, 1)], Y, 0, *NORTH)
    y_flags = send(flags.at[:, ylast], FL.at[xown, ylow], Y, 1, *NORTH)
    y_cells = [
        send(flags.at[:, yfirst], FL.at[xown, yhigh], Y, 2, *SOUTH),
        send(visc.at[:, ylast], VI.at[xown, ylow], Y, 3, *NORTH),
        send(visc.at[:, yfirst], VI.at[xown, yhigh], Y, 4, *SOUTH),
    ]

    for copy in local[:3]:
        copy.wait()
    y_press()
    y_flags()
    y_cells.pop(0)()

    def is_fluid(f):
        return jnp.where(f == 1, 1.0, 0.0)

    def is_open(f):
        return jnp.where(f != 0, 1.0, 0.0)

    for a, b in blocks(X0, X1, 4):
        f = FL[a:b]
        fluid, opened = is_fluid(f), is_open(f)
        p = PR[a - LOW + 1 : b - LOW + 1] * fluid
        act = jnp.maximum(fluid, low_y(fluid)) * opened * low_y(opened)
        S[1, a:b, Y0:Y1] = (act * (VEL[1, a - X0 : b - X0] - (p - low_y(p))))[:, Y0:Y1]
        act = jnp.maximum(fluid, low_z(fluid)) * opened * low_z(opened)
        S[2, a:b, Y0:Y1] = (act * (VEL[2, a - X0 : b - X0] - (p - low_z(p))))[:, Y0:Y1]
        if a == X0:
            RAW[...] = VEL[0, 0:1] - p[0:1]
            fluid, opened, p, a = fluid[1:], opened[1:], p[1:], a + 1
        below = FL[a - 1 : b - 1]
        fluid_below = is_fluid(below)
        p_below = PR[a - LOW : b - LOW] * fluid_below
        act = jnp.maximum(fluid, fluid_below) * opened * is_open(below)
        S[0, a:b, Y0:Y1] = (act * (VEL[0, a - X0 : b - X0] - (p - p_below)))[:, Y0:Y1]

    vw = pl.ds(1, 2)
    x_started = [
        send(S.at[:, pl.ds(X1 - LOW, LOW), rows], S.at[:, xlow, rows], X, 5, *UP),
        send(S.at[vw, pl.ds(X0, HIGH), rows], S.at[vw, xhigh, rows], X, 6, *DOWN),
        send(S.at[0, pl.ds(X0 + 1, HIGH - 1), rows], S.at[0, pl.ds(X1 + 1, HIGH - 1), rows], X, 7, *DOWN),
        send(RAW.at[:, rows], RAWIN.at[:, rows], X, 8, *DOWN),
    ]
    upper = pl.ds(X0 + 1, NX - 1)
    y_started = [
        send(S.at[vw, xown, elast], S.at[vw, xown, ylow], Y, 5, *NORTH),
        send(S.at[0, upper, elast], S.at[0, upper, ylow], Y, 6, *NORTH),
        send(S.at[vw, xown, efirst], S.at[vw, xown, yhigh], Y, 7, *SOUTH),
        send(S.at[0, upper, efirst], S.at[0, upper, yhigh], Y, 8, *SOUTH),
    ]

    local[3].wait()
    n = 9
    for wait in x_cells:
        wait()
    for ref in (FL, VI):
        for layers in (xlow, xhigh):
            y_cells.append(send(ref.at[layers, elast], ref.at[layers, ylow], Y, n, *NORTH))
            y_cells.append(send(ref.at[layers, efirst], ref.at[layers, yhigh], Y, n + 1, *SOUTH))
            n += 2
    for wait in y_cells:
        wait()

    for a, b in blocks(1, EX, 5):
        f = is_fluid(FL[a - 1 : b])
        m = VI[a - 1 : b]
        fx, mx = jnp.maximum(f[1:], f[:-1]), m[1:] + m[:-1]
        fc, mc = f[1:], m[1:]
        if a == 1:
            CW[0] = 2.0 * m[0] * f[0]
        CW[a:b] = 2.0 * mc * fc
        WXY[a:b] = 0.25 * (mx + low_y(mx)) * jnp.maximum(fx, low_y(fx))
        WXZ[a:b] = 0.25 * (mx + low_z(mx)) * jnp.maximum(fx, low_z(fx))
        fy, my = jnp.maximum(fc, low_y(fc)), mc + low_y(mc)
        WYZ[a:b] = 0.25 * (my + low_z(my)) * jnp.maximum(fy, low_z(fy))
        top = lanes(fx) == NZ - 1
        EU[a:b] = jnp.where(top, 0.25 * mx * fx, 0.0)
        EV[a:b] = jnp.where(top, 0.25 * my * fy, 0.0)
    for a, b in blocks(1, EX - 1, 5):
        f = FL[a - 1 : b]
        fluid, opened = is_fluid(f), is_open(f)
        fc, oc = fluid[1:], opened[1:]
        cw = CW[a:b]
        wxy, wxz, wyz = WXY[a : b + 1], WXZ[a : b + 1], WYZ[a:b]
        xy, xz = wxy[:-1], wxz[:-1]
        act = jnp.maximum(fc, fluid[:-1]) * oc * opened[:-1]
        DU[a:b] = act / (1.0 + cw + CW[a - 1 : b - 1] + xy + next_y(xy) + xz + next_z(xz) + EU[a:b])
        act = jnp.maximum(fc, low_y(fc)) * oc * low_y(oc)
        DV[a:b] = act / (1.0 + cw + low_y(cw) + xy + wxy[1:] + wyz + next_z(wyz) + EV[a:b])
        act = jnp.maximum(fc, low_z(fc)) * oc * low_z(oc)
        DW[a:b] = act / (1.0 + cw + low_z(cw) + xz + wxz[1:] + wyz + next_y(wyz))

    for wait in x_started:
        wait()
    x_press()
    for layer, below, raw in ((X0, PR[0:1], RAW[...]), (X1, PR[NX : NX + 1], RAWIN[...])):
        f, g = FL[layer : layer + 1], FL[layer - 1 : layer]
        act = jnp.maximum(is_fluid(f), is_fluid(g)) * is_open(f) * is_open(g)
        S[0, layer : layer + 1, Y0:Y1] = (act * (raw + below * is_fluid(g)))[:, Y0:Y1]
    lowest = pl.ds(X0, 1)
    for there, at in ((S, (slice(None), xlow)), (S, (slice(None), xhigh)), (S, (0, lowest))):
        y_started.append(send(there.at[(*at, elast)], there.at[(*at, ylow)], Y, n, *NORTH))
        y_started.append(send(there.at[(*at, efirst)], there.at[(*at, yhigh)], Y, n + 1, *SOUTH))
        n += 2
    for wait in y_started:
        wait()

    def gradient(F, a, b):
        u, v, w = F[0, a - 1 : b + 1], F[1, a - 1 : b + 1], F[2, a - 1 : b + 1]
        uc, vc, wc = u[1:-1], v[1:-1], w[1:-1]
        sx = CW[a - 1 : b] * (u[1:] - u[:-1])
        un, vn, wn = u[1:], v[1:], w[1:]
        xy = WXY[a : b + 1] * (un - low_y(un) + vn - v[:-1])
        xz = WXZ[a : b + 1] * (un - low_z(un) + wn - w[:-1])
        cw = CW[a:b]
        sy = cw * (next_y(vc) - vc)
        sz = cw * (next_z(wc) - wc)
        yz = WYZ[a:b] * (vc - low_z(vc) + wc - low_y(wc))
        xyc, xzc = xy[:-1], xz[:-1]
        return (
            sx[:-1] - sx[1:] + xyc - next_y(xyc) + xzc - next_z(xzc) + EU[a:b] * uc,
            low_y(sy) - sy + xyc - xy[1:] + yz - next_z(yz) + EV[a:b] * vc,
            low_z(sz) - sz + xzc - xz[1:] + yz - next_y(yz),
        ), (uc, vc, wc)

    D = (DU, DV, DW)
    row = lax.broadcasted_iota(jnp.int32, (1, EY, NZ), 1)
    inside = (row >= Y0) & (row < Y1)

    def partial(values, a, b, mask):
        lo, hi = max(a, X0), min(b, X1)
        if lo >= hi:
            return jnp.zeros((1, EY, NZ), F32)
        part = values[lo - a : hi - a]
        return jnp.where(mask, jnp.sum(part, axis=0, keepdims=True), 0.0)

    zero = jnp.zeros((1, EY, NZ), F32)
    b0 = h00 = h01 = h11 = h12 = h22 = zero
    for a, b in blocks(1, EX - 1, 4):
        grad, _ = gradient(S, a, b)
        total = 0.0
        for c in range(3):
            z = -D[c][a:b] * grad[c]
            V0[c, a:b] = z
            total = total - z * grad[c]
        b0 = b0 + partial(total, a, b, inside)
    for a, b in blocks(2, EX - 2, 4):
        grad, field = gradient(V0, a, b)
        same = cross = 0.0
        for c in range(3):
            g = field[c] + grad[c]
            z = D[c][a:b] * g - field[c]
            V1[c, a:b] = z
            same, cross = same + field[c] * g, cross + z * g
        h00, h01 = h00 + partial(same, a, b, inside), h01 + partial(cross, a, b, inside)
    for a, b in blocks(3, EX - 3, 4):
        grad, field = gradient(V1, a, b)
        same = cross = 0.0
        for c in range(3):
            g = field[c] + grad[c]
            z = D[c][a:b] * g - field[c]
            V2[c, a:b] = z
            same, cross = same + field[c] * g, cross + z * g
        h11, h12 = h11 + partial(same, a, b, inside), h12 + partial(cross, a, b, inside)
    edge = row == Y1
    upto = inside | (edge & jnp.logical_not(has_yhi))
    below = ((row >= Y0 - 1) & (row < Y1 - 1)) | ((row == Y1 - 1) & jnp.logical_not(has_yhi))
    for a, b in blocks(X0, X1 + 1, 5):
        u, v, w = V2[0, a - 1 : b], V2[1, a - 1 : b], V2[2, a - 1 : b]
        uc, vc, wc = u[1:], v[1:], w[1:]
        cw = CW[a - 1 : b]
        dx = uc - u[:-1]
        xy = uc - low_y(uc) + vc - v[:-1]
        xz = uc - low_z(uc) + wc - w[:-1]
        yz = vc - low_z(vc) + wc - low_y(wc)
        dz = next_z(wc) - wc
        dy = next_y(vc) - vc
        most = (
            cw[:-1] * dx * dx + WXY[a:b] * xy * xy + WXZ[a:b] * xz * xz + WYZ[a:b] * yz * yz
            + cw[1:] * dz * dz + (1.0 + EU[a:b]) * uc * uc + (1.0 + EV[a:b]) * vc * vc + wc * wc
        )
        along = cw[1:] * dy * dy
        value = jnp.where(upto, most, 0.0) + jnp.where(below, along, 0.0)
        h22 = h22 + jnp.sum(value[: min(b, X1) - a], axis=0, keepdims=True)
        if b > X1:
            h22 = h22 + jnp.where(has_xhi, 0.0, value[X1 - a : X1 - a + 1])

    lane = lax.broadcasted_iota(jnp.int32, (1, NZ), 1)
    payload = jnp.zeros((1, NZ), F32)
    for k, value in enumerate((b0, h00, h01, h11, h12, h22)):
        total = jnp.sum(jnp.sum(value[0], axis=0, keepdims=True), axis=1, keepdims=True)
        payload = jnp.where(lane == k, total, payload)

    def gather(slots, count, me, device, sends, recvs, value):
        slots[me] = value
        copy = lambda peer: pltpu.make_async_remote_copy(
            src_ref=slots.at[me], dst_ref=slots.at[me], send_sem=sends.at[peer], recv_sem=recvs.at[me],
            device_id=device(peer), device_id_type=MESH,
        )
        arrival = lambda peer: pltpu.make_async_remote_copy(
            src_ref=slots.at[me], dst_ref=slots.at[peer], send_sem=sends.at[peer], recv_sem=recvs.at[peer],
            device_id=device(peer), device_id_type=MESH,
        )

        @pl.loop(1, count)
        def _(d):
            copy(lax.rem(me + d, count)).start()

        @pl.loop(1, count)
        def _(d):
            arrival(lax.rem(me + d, count)).wait_recv()

        def finish():
            @pl.loop(1, count)
            def _(d):
                copy(lax.rem(me + d, count)).wait_send()

        total = slots[0]
        for r in range(1, count):
            total = total + slots[r]
        return total, finish

    total, finish_cards = gather(CARDS, CARD, card, card_device, cs, cr, payload)
    total, finish_rings = gather(RINGS, RING, ring, ring_device, rs, rr, total)

    wide = jnp.broadcast_to(total, (8, NZ))
    at = lax.broadcasted_iota(jnp.int32, (8, NZ), 1)
    m = [
        jnp.broadcast_to(jnp.sum(jnp.where(at == k, wide, 0.0), axis=1, keepdims=True), (8, NZ))
        for k in range(6)
    ]
    r0, a00, a01, a11, a12, a22 = m
    r1 = a00 - r0
    r2 = a01 - r1
    a02 = a11
    tiny = 1e-6

    def over(top, pivot, size):
        good = pivot > tiny * size
        return jnp.where(good, top / jnp.where(good, pivot, 1.0), 0.0)

    d0 = a00
    l10, l20 = over(a01, d0, 0.0), over(a02, d0, 0.0)
    d1 = a11 - l10 * a01
    e21 = a12 - l20 * a01
    l21 = over(e21, d1, a11)
    d2 = a22 - l20 * a02 - l21 * e21
    y1 = r1 - l10 * r0
    y2 = r2 - l20 * r0 - l21 * y1
    c2 = over(y2, d2, a22)
    c1 = over(y1, d1, a11) - l21 * c2
    c0 = over(r0, d0, 0.0) - l10 * c1 - l20 * c2
    c0, c1, c2 = c0[0:1], c1[0:1], c2[0:1]
    for c in range(3):
        for a, b in blocks(X0, X1, 4):
            out[c, a - X0 : b - X0] = (
                S[c, a:b, Y0:Y1] + c0 * V0[c, a:b, Y0:Y1] + c1 * V1[c, a:b, Y0:Y1] + c2 * V2[c, a:b, Y0:Y1]
            )
    for there, copy in sent:
        pl.when(there)(copy.wait_send)
    finish_cards()
    finish_rings()


def solution(mesh):
    gxn, gyn = mesh.shape["gx"], mesh.shape["gy"]
    block, cells = P(None, "gx", "gy", None), P("gx", "gy", None)
    ext = (EX, EY, NZ)
    field = lambda *shape: pltpu.VMEM(shape, F32)
    dma = lambda n: pltpu.SemaphoreType.DMA((n,))

    def local(velocity, viscosity, pressure, flags):
        def body(*refs):
            kernel(gxn, gyn, *refs)

        return pl.pallas_call(
            body,
            out_shape=jax.ShapeDtypeStruct((3, NX, NY, NZ), F32),
            in_specs=[pl.BlockSpec(memory_space=pl.ANY)] * 4,
            out_specs=pl.BlockSpec(memory_space=pltpu.VMEM),
            scratch_shapes=[
                *[field(3, *ext)] * 4, field(3, NX, EY, NZ), field(*ext), pltpu.VMEM(ext, jnp.int32),
                field(NX + 1, EY, NZ), field(1, EY, NZ), field(1, EY, NZ),
                *[field(*ext)] * 9,
                field(CARD, 1, NZ), field(RING, 1, NZ),
                dma(4), dma(9), dma(9), dma(23), dma(23), dma(CARD), dma(CARD), dma(RING), dma(RING),
            ],
            compiler_params=pltpu.CompilerParams(
                collective_id=1, has_side_effects=True, vmem_limit_bytes=48 * 2**20
            ),
        )(velocity, viscosity, pressure, flags)

    return jax.shard_map(local, mesh=mesh, in_specs=(block, cells, cells, cells), out_specs=block, check_vma=False)
```

```python
import jax
import jax.numpy as jnp
from jax import lax
from jax.experimental import pallas as pl
from jax.experimental.pallas import tpu as pltpu
from jax.sharding import PartitionSpec as P

MESH = pl.DeviceIdType.MESH
F32 = jnp.float32
NX, NY, NZ = 8, 16, 128
LOW, HIGH = 4, 3
EX, EY = NX + LOW + HIGH, 24
X0, X1 = LOW, LOW + NX
Y0, Y1 = LOW, LOW + NY
CARD, RING = 32, 16


def low_y(a):
    return pltpu.roll(a, 1, 1)


def next_y(a):
    return pltpu.roll(a, EY - 1, 1)


def lanes(a):
    return lax.broadcasted_iota(jnp.int32, a.shape, a.ndim - 1)


def low_z(a):
    return jnp.where(lanes(a) == 0, 0.0, pltpu.roll(a, 1, a.ndim - 1))


def next_z(a):
    return jnp.where(lanes(a) == NZ - 1, 0.0, pltpu.roll(a, NZ - 1, a.ndim - 1))


def blocks(start, stop, size):
    count = -(-(stop - start) // size)
    edges = [start + (stop - start) * n // count for n in range(count + 1)]
    return list(zip(edges[:-1], edges[1:]))


def kernel(
    gxn, gyn,
    vel, visc, press, flags, out,
    S, V0, V1, V2, VEL, VI, FL, PR, RAW, RAWIN, VIA, FLA,
    CW, WXY, WXZ, WYZ, EU, EV, DU, DV, DW,
    CARDS, RINGS,
    lsem, xs, xr, ys, yr, gs, gr,
):
    gx, gy = lax.axis_index("gx"), lax.axis_index("gy")
    has_xlo, has_xhi = gx > 0, gx < gxn - 1
    has_ylo, has_yhi = gy > 0, gy < gyn - 1
    xlo, xhi = (gx - 1, gy), (gx + 1, gy)
    ylo, yhi = (gx, gy - 1), (gx, gy + 1)
    px, zh, py = gx // 8, lax.rem(gx // 4, 2), lax.rem(gx, 4)
    zl, core = gy // 2, lax.rem(gy, 2)
    card = (px * 4 + py) * 2 + core
    ring = zh * 8 + zl

    def hops(d, n):
        return min(d, n - d)

    steps = [(dx, dy, dc) for dx in range(4) for dy in range(4) for dc in range(2)]
    steps.sort(key=lambda d: -(hops(d[0], 4) + hops(d[1], 4) + 0.3 * d[2]))
    pxs, pys, cores = [lax.rem(px + d, 4) * 8 for d in range(4)], [lax.rem(py + d, 4) for d in range(4)], (core, 1 - core)
    card_peers = [(pxs[dx] + zh * 4 + pys[dy], zl * 2 + cores[dc]) for dx, dy, dc in steps[:-1]]
    ring_peers = []
    for d in sorted(range(1, RING), key=lambda d: -hops(d, RING)):
        z = lax.rem(ring + d, RING)
        ring_peers.append((px * 8 + (z // 8) * 4 + py, lax.rem(z, 8) * 2 + core))

    own = (pl.ds(X0, NX), pl.ds(Y0, NY))
    local = [
        pltpu.make_async_copy(flags, FL.at[own], lsem.at[0]),
        pltpu.make_async_copy(press, PR.at[pl.ds(1, NX), pl.ds(Y0, NY)], lsem.at[1]),
        pltpu.make_async_copy(vel, VEL, lsem.at[2]),
        pltpu.make_async_copy(visc, VI.at[own], lsem.at[3]),
    ]
    for copy in local:
        copy.start()

    def clear(ref, lead, kind):
        zero = lambda *shape: jnp.zeros(shape, kind)
        for c in range(lead) if lead else [None]:
            at = ref if c is None else ref.at[c]
            at[0:X0] = zero(X0, EY, NZ)
            at[X1:EX] = zero(EX - X1, EY, NZ)
            at[X0:X1, 0:Y0] = zero(NX, Y0, NZ)
            at[X0:X1, Y1:EY] = zero(NX, EY - Y1, NZ)

    clear(S, 3, F32)
    clear(VI, 0, F32)
    clear(FL, 0, jnp.int32)
    PR[0] = jnp.zeros((EY, NZ), F32)
    PR[1:, 0:Y0] = jnp.zeros((NX, Y0, NZ), F32)
    PR[1:, Y1:EY] = jnp.zeros((NX, EY - Y1, NZ), F32)
    RAWIN[...] = jnp.zeros((1, NY, NZ), F32)
    for c in range(3):
        V2[c, X1] = jnp.zeros((EY, NZ), F32)

    barrier = pltpu.get_barrier_semaphore()

    def greet(device):
        pl.semaphore_signal(barrier, inc=1, device_id=device, device_id_type=MESH)

    far_up = (py == 3) & has_xhi
    relay = (py == 2) & (gx < gxn - 2)
    far_down = (py == 0) & has_xlo
    near = [
        (has_xlo, xlo), (has_xhi, xhi), (has_ylo, ylo), (has_yhi, yhi),
        (relay, (gx + 2, gy)), (far_down, (gx - 2, gy)),
    ]
    for there, device in near:
        pl.when(there)(lambda device=device: greet(device))

    for device in ring_peers + card_peers:
        greet(device)

    def is_fluid(f):
        return jnp.where(f == 1, 1.0, 0.0)

    def is_open(f):
        return jnp.where(f != 0, 1.0, 0.0)

    def pressed(a, b, y):
        f = FL[a:b, y : y + NY]
        fluid = is_fluid(f)
        return fluid, is_open(f), PR[a - LOW + 1 : b - LOW + 1, y : y + NY] * fluid

    for copy in local[:3]:
        copy.wait()
    for a, b in blocks(X0, X1, 2):
        fluid, opened, p = pressed(a, b, Y0)
        act = jnp.maximum(fluid, low_z(fluid)) * opened * low_z(opened)
        S[2, a:b, Y0:Y1] = act * (VEL[2, a - X0 : b - X0] - (p - low_z(p)))
        if a == X0:
            RAW[...] = VEL[0, 0:1] - p[0:1]
            fluid, opened, p, a = fluid[1:], opened[1:], p[1:], a + 1
        fluid_low, opened_low, p_low = pressed(a - 1, b - 1, Y0)
        act = jnp.maximum(fluid, fluid_low) * opened * opened_low
        S[0, a:b, Y0:Y1] = act * (VEL[0, a - X0 : b - X0] - (p - p_low))

    one = lambda there: jnp.where(there, 1, 0)
    pl.semaphore_wait(barrier, CARD + RING - 2 + sum(one(t) for t, _ in near))

    sent = []

    def send(source, target, sems, n, to, there, from_, out=None):
        copy = pltpu.make_async_remote_copy(
            src_ref=source, dst_ref=target, send_sem=sems[0].at[n if out is None else out], recv_sem=sems[1].at[n],
            device_id=to, device_id_type=MESH,
        )
        pl.when(there)(copy.start)
        sent.append((there, copy))
        return lambda: pl.when(from_)(copy.wait_recv)

    X, Y = (xs, xr), (ys, yr)
    UP, DOWN = (xhi, has_xhi, has_xlo), (xlo, has_xlo, has_xhi)
    NORTH, SOUTH = (yhi, has_yhi, has_ylo), (ylo, has_ylo, has_yhi)
    rows = pl.ds(Y0, NY)
    last4, first3 = pl.ds(NX - LOW, LOW), pl.ds(0, HIGH)
    xlow, xhigh, xown = pl.ds(0, LOW), pl.ds(X1, HIGH), pl.ds(X0, NX)
    ylow, yhigh = pl.ds(0, LOW), pl.ds(Y1, HIGH)
    ylast, yfirst = pl.ds(NY - LOW, LOW), pl.ds(0, HIGH)
    elast, efirst = pl.ds(Y1 - LOW, LOW), pl.ds(Y0, HIGH)

    u, v, w = 0, 1, 2
    upper = pl.ds(X0 + 1, NX - 1)
    top4, low3 = pl.ds(X1 - LOW, LOW), pl.ds(X0, HIGH)
    far_cells = [
        send(source.at[last4], target, X, n, xlo, far_up, relay)
        for n, source, target in ((9, visc, VIA), (10, flags, FLA))
    ]
    direct_up = has_xhi & (py != 3)
    x_started = [
        send(S.at[u, top4, rows], S.at[u, xlow, rows], X, 5, *UP),
        send(S.at[w, top4, rows], S.at[w, xlow, rows], X, 6, *UP),
        send(RAW, RAWIN, X, 8, *DOWN),
        send(S.at[u, pl.ds(X0 + 1, HIGH - 1), rows], S.at[u, pl.ds(X1 + 1, HIGH - 1), rows], X, 7, *DOWN),
        send(S.at[w, low3, rows], S.at[w, xhigh, rows], X, 11, *DOWN),
    ]
    y_press = send(press.at[:, pl.ds(NY - 1, 1)], PR.at[pl.ds(1, NX), pl.ds(Y0 - 1, 1)], Y, 0, *NORTH)
    y_flags = send(flags.at[:, ylast], FL.at[xown, ylow], Y, 1, *NORTH)
    x_flags = send(flags.at[first3], FL.at[xhigh, rows], X, 1, *DOWN)
    x_visc = send(visc.at[first3], VI.at[xhigh, rows], X, 3, *DOWN)
    x_press = send(press.at[pl.ds(NX - 1, 1)], PR.at[pl.ds(0, 1), rows], X, 4, *UP)
    x_cells = [
        send(flags.at[last4], FL.at[xlow, rows], X, 0, xhi, direct_up, has_xlo),
        x_flags,
        send(visc.at[last4], VI.at[xlow, rows], X, 2, xhi, direct_up, has_xlo),
        x_visc,
    ]
    y_cells = [
        send(flags.at[:, yfirst], FL.at[xown, yhigh], Y, 2, *SOUTH),
        send(visc.at[:, ylast], VI.at[xown, ylow], Y, 3, *NORTH),
        send(visc.at[:, yfirst], VI.at[xown, yhigh], Y, 4, *SOUTH),
    ]
    y_started = [
        send(S.at[w, xown, elast], S.at[w, xown, ylow], Y, 5, *NORTH),
        send(S.at[u, upper, elast], S.at[u, upper, ylow], Y, 6, *NORTH),
        send(S.at[w, xown, efirst], S.at[w, xown, yhigh], Y, 7, *SOUTH),
        send(S.at[u, upper, efirst], S.at[u, upper, yhigh], Y, 8, *SOUTH),
    ]

    y_press()
    y_flags()
    for a, b in blocks(X0, X1, 2):
        fluid, opened, p = pressed(a, b, Y0)
        fluid_low, opened_low, p_low = pressed(a, b, Y0 - 1)
        act = jnp.maximum(fluid, fluid_low) * opened * opened_low
        S[1, a:b, Y0:Y1] = act * (VEL[1, a - X0 : b - X0] - (p - p_low))
    x_started += [
        send(S.at[v, top4, rows], S.at[v, xlow, rows], X, 12, *UP),
        send(S.at[v, low3, rows], S.at[v, xhigh, rows], X, 13, *DOWN),
    ]
    y_started += [
        send(S.at[v, xown, elast], S.at[v, xown, ylow], Y, 9, *NORTH),
        send(S.at[v, xown, efirst], S.at[v, xown, yhigh], Y, 10, *SOUTH),
    ]
    for wait in far_cells:
        wait()
    for n, source, target in ((2, VIA, VI), (0, FLA, FL)):
        send(source, target.at[xlow, rows], X, n, (gx + 2, gy), relay, None, out=14 + n // 2)

    local[3].wait()
    n = 11
    for wait in x_cells:
        wait()
    for ref in (FL, VI):
        for layers in (xlow, xhigh):
            y_cells.append(send(ref.at[layers, elast], ref.at[layers, ylow], Y, n, *NORTH))
            y_cells.append(send(ref.at[layers, efirst], ref.at[layers, yhigh], Y, n + 1, *SOUTH))
            n += 2
    for wait in y_cells:
        wait()

    for a, b in blocks(1, EX, 5):
        f = is_fluid(FL[a - 1 : b])
        m = VI[a - 1 : b]
        fx, mx = jnp.maximum(f[1:], f[:-1]), m[1:] + m[:-1]
        fc, mc = f[1:], m[1:]
        if a == 1:
            CW[0] = 2.0 * m[0] * f[0]
        CW[a:b] = 2.0 * mc * fc
        WXY[a:b] = 0.25 * (mx + low_y(mx)) * jnp.maximum(fx, low_y(fx))
        WXZ[a:b] = 0.25 * (mx + low_z(mx)) * jnp.maximum(fx, low_z(fx))
        fy, my = jnp.maximum(fc, low_y(fc)), mc + low_y(mc)
        WYZ[a:b] = 0.25 * (my + low_z(my)) * jnp.maximum(fy, low_z(fy))
        top = lanes(fx) == NZ - 1
        EU[a:b] = jnp.where(top, 0.25 * mx * fx, 0.0)
        EV[a:b] = jnp.where(top, 0.25 * my * fy, 0.0)
    for a, b in blocks(1, EX - 1, 5):
        f = FL[a - 1 : b]
        fluid, opened = is_fluid(f), is_open(f)
        fc, oc = fluid[1:], opened[1:]
        cw = CW[a:b]
        wxy, wxz, wyz = WXY[a : b + 1], WXZ[a : b + 1], WYZ[a:b]
        xy, xz = wxy[:-1], wxz[:-1]
        act = jnp.maximum(fc, fluid[:-1]) * oc * opened[:-1]
        DU[a:b] = act / (1.0 + cw + CW[a - 1 : b - 1] + xy + next_y(xy) + xz + next_z(xz) + EU[a:b])
        act = jnp.maximum(fc, low_y(fc)) * oc * low_y(oc)
        DV[a:b] = act / (1.0 + cw + low_y(cw) + xy + wxy[1:] + wyz + next_z(wyz) + EV[a:b])
        act = jnp.maximum(fc, low_z(fc)) * oc * low_z(oc)
        DW[a:b] = act / (1.0 + cw + low_z(cw) + xz + wxz[1:] + wyz + next_y(wyz))

    for wait in x_started:
        wait()
    x_press()
    for layer, below, raw in ((X0, 0, RAW), (X1, NX, RAWIN)):
        f, g = FL[layer : layer + 1, Y0:Y1], FL[layer - 1 : layer, Y0:Y1]
        act = jnp.maximum(is_fluid(f), is_fluid(g)) * is_open(f) * is_open(g)
        S[0, layer : layer + 1, Y0:Y1] = act * (raw[...] + PR[below : below + 1, Y0:Y1] * is_fluid(g))
    lowest = pl.ds(X0, 1)
    for there, at in ((S, (slice(None), xlow)), (S, (slice(None), xhigh)), (S, (0, lowest))):
        y_started.append(send(there.at[(*at, elast)], there.at[(*at, ylow)], Y, n, *NORTH))
        y_started.append(send(there.at[(*at, efirst)], there.at[(*at, yhigh)], Y, n + 1, *SOUTH))
        n += 2
    for wait in y_started:
        wait()

    def gradient(F, a, b):
        u, v, w = F[0, a - 1 : b + 1], F[1, a - 1 : b + 1], F[2, a - 1 : b + 1]
        uc, vc, wc = u[1:-1], v[1:-1], w[1:-1]
        sx = CW[a - 1 : b] * (u[1:] - u[:-1])
        un, vn, wn = u[1:], v[1:], w[1:]
        xy = WXY[a : b + 1] * (un - low_y(un) + vn - v[:-1])
        xz = WXZ[a : b + 1] * (un - low_z(un) + wn - w[:-1])
        cw = CW[a:b]
        sy = cw * (next_y(vc) - vc)
        sz = cw * (next_z(wc) - wc)
        yz = WYZ[a:b] * (vc - low_z(vc) + wc - low_y(wc))
        xyc, xzc = xy[:-1], xz[:-1]
        return (
            sx[:-1] - sx[1:] + xyc - next_y(xyc) + xzc - next_z(xzc) + EU[a:b] * uc,
            low_y(sy) - sy + xyc - xy[1:] + yz - next_z(yz) + EV[a:b] * vc,
            low_z(sz) - sz + xzc - xz[1:] + yz - next_y(yz),
        ), (uc, vc, wc)

    D = (DU, DV, DW)
    row = lax.broadcasted_iota(jnp.int32, (1, EY, NZ), 1)
    inside = (row >= Y0) & (row < Y1)

    def partial(values, a, b, mask):
        lo, hi = max(a, X0), min(b, X1)
        if lo >= hi:
            return jnp.zeros((1, EY, NZ), F32)
        part = values[lo - a : hi - a]
        return jnp.where(mask, jnp.sum(part, axis=0, keepdims=True), 0.0)

    zero = jnp.zeros((1, EY, NZ), F32)
    b0 = h00 = h01 = h11 = h12 = h22 = zero
    for a, b in blocks(1, EX - 1, 4):
        grad, _ = gradient(S, a, b)
        total = 0.0
        for c in range(3):
            z = -D[c][a:b] * grad[c]
            V0[c, a:b] = z
            total = total - z * grad[c]
        b0 = b0 + partial(total, a, b, inside)
    for a, b in blocks(2, EX - 2, 4):
        grad, field = gradient(V0, a, b)
        same = cross = 0.0
        for c in range(3):
            g = field[c] + grad[c]
            z = D[c][a:b] * g - field[c]
            V1[c, a:b] = z
            same, cross = same + field[c] * g, cross + z * g
        h00, h01 = h00 + partial(same, a, b, inside), h01 + partial(cross, a, b, inside)
    for a, b in blocks(3, EX - 3, 4):
        grad, field = gradient(V1, a, b)
        same = cross = 0.0
        for c in range(3):
            g = field[c] + grad[c]
            z = D[c][a:b] * g - field[c]
            V2[c, a:b] = z
            same, cross = same + field[c] * g, cross + z * g
        h11, h12 = h11 + partial(same, a, b, inside), h12 + partial(cross, a, b, inside)
    edge = row == Y1
    upto = inside | (edge & jnp.logical_not(has_yhi))
    below = ((row >= Y0 - 1) & (row < Y1 - 1)) | ((row == Y1 - 1) & jnp.logical_not(has_yhi))
    for a, b in blocks(X0, X1 + 1, 5):
        u, v, w = V2[0, a - 1 : b], V2[1, a - 1 : b], V2[2, a - 1 : b]
        uc, vc, wc = u[1:], v[1:], w[1:]
        cw = CW[a - 1 : b]
        dx = uc - u[:-1]
        xy = uc - low_y(uc) + vc - v[:-1]
        xz = uc - low_z(uc) + wc - w[:-1]
        yz = vc - low_z(vc) + wc - low_y(wc)
        dz = next_z(wc) - wc
        dy = next_y(vc) - vc
        most = (
            cw[:-1] * dx * dx + WXY[a:b] * xy * xy + WXZ[a:b] * xz * xz + WYZ[a:b] * yz * yz
            + cw[1:] * dz * dz + (1.0 + EU[a:b]) * uc * uc + (1.0 + EV[a:b]) * vc * vc + wc * wc
        )
        along = cw[1:] * dy * dy
        value = jnp.where(upto, most, 0.0) + jnp.where(below, along, 0.0)
        h22 = h22 + jnp.sum(value[: min(b, X1) - a], axis=0, keepdims=True)
        if b > X1:
            h22 = h22 + jnp.where(has_xhi, 0.0, value[X1 - a : X1 - a + 1])

    lane = lax.broadcasted_iota(jnp.int32, (1, NZ), 1)
    payload = jnp.zeros((1, NZ), F32)
    for k, value in enumerate((b0, h00, h01, h11, h12, h22)):
        total = jnp.sum(jnp.sum(value[0], axis=0, keepdims=True), axis=1, keepdims=True)
        payload = jnp.where(lane == k, total, payload)

    def gather(slots, me, peers, n, value):
        slots[me] = value
        for device in peers:
            pltpu.make_async_remote_copy(
                src_ref=slots.at[me], dst_ref=slots.at[me], send_sem=gs.at[n], recv_sem=gr.at[n],
                device_id=device, device_id_type=MESH,
            ).start()
        rest = slots.at[pl.ds(0, len(peers))]
        every = pltpu.make_async_remote_copy(
            src_ref=rest, dst_ref=rest, send_sem=gs.at[n], recv_sem=gr.at[n],
            device_id=peers[0], device_id_type=MESH,
        )
        every.wait_recv()
        total = slots[0]
        for r in range(1, len(peers) + 1):
            total = total + slots[r]
        return total, every.wait_send

    total, finish_cards = gather(CARDS, card, card_peers, 0, payload)
    total, finish_rings = gather(RINGS, ring, ring_peers, 1, total)

    wide = jnp.broadcast_to(total, (8, NZ))
    at = lax.broadcasted_iota(jnp.int32, (8, NZ), 1)
    m = [
        jnp.broadcast_to(jnp.sum(jnp.where(at == k, wide, 0.0), axis=1, keepdims=True), (8, NZ))
        for k in range(6)
    ]
    r0, a00, a01, a11, a12, a22 = m
    r1 = a00 - r0
    r2 = a01 - r1
    a02 = a11
    tiny = 1e-6

    def over(top, pivot, size):
        good = pivot > tiny * size
        return jnp.where(good, top / jnp.where(good, pivot, 1.0), 0.0)

    d0 = a00
    l10, l20 = over(a01, d0, 0.0), over(a02, d0, 0.0)
    d1 = a11 - l10 * a01
    e21 = a12 - l20 * a01
    l21 = over(e21, d1, a11)
    d2 = a22 - l20 * a02 - l21 * e21
    y1 = r1 - l10 * r0
    y2 = r2 - l20 * r0 - l21 * y1
    c2 = over(y2, d2, a22)
    c1 = over(y1, d1, a11) - l21 * c2
    c0 = over(r0, d0, 0.0) - l10 * c1 - l20 * c2
    c0, c1, c2 = c0[0:1], c1[0:1], c2[0:1]
    for c in range(3):
        for a, b in blocks(X0, X1, 4):
            out[c, a - X0 : b - X0] = (
                S[c, a:b, Y0:Y1] + c0 * V0[c, a:b, Y0:Y1] + c1 * V1[c, a:b, Y0:Y1] + c2 * V2[c, a:b, Y0:Y1]
            )
    for there, copy in sent:
        pl.when(there)(copy.wait_send)
    finish_cards()
    finish_rings()


def solution(mesh):
    gxn, gyn = mesh.shape["gx"], mesh.shape["gy"]
    block, cells = P(None, "gx", "gy", None), P("gx", "gy", None)
    ext = (EX, EY, NZ)
    field = lambda *shape: pltpu.VMEM(shape, F32)
    dma = lambda n: pltpu.SemaphoreType.DMA((n,))

    def local(velocity, viscosity, pressure, flags):
        def body(*refs):
            kernel(gxn, gyn, *refs)

        return pl.pallas_call(
            body,
            out_shape=jax.ShapeDtypeStruct((3, NX, NY, NZ), F32),
            in_specs=[pl.BlockSpec(memory_space=pl.ANY)] * 4,
            out_specs=pl.BlockSpec(memory_space=pltpu.VMEM),
            scratch_shapes=[
                *[field(3, *ext)] * 4, field(3, NX, NY, NZ), field(*ext), pltpu.VMEM(ext, jnp.int32),
                field(NX + 1, EY, NZ), field(1, NY, NZ), field(1, NY, NZ),
                field(LOW, NY, NZ), pltpu.VMEM((LOW, NY, NZ), jnp.int32),
                *[field(*ext)] * 9,
                field(CARD, 1, NZ), field(RING, 1, NZ),
                dma(4), dma(16), dma(14), dma(25), dma(25), dma(2), dma(2),
            ],
            compiler_params=pltpu.CompilerParams(
                collective_id=1, has_side_effects=True, vmem_limit_bytes=60 * 2**20
            ),
        )(velocity, viscosity, pressure, flags)

    return jax.shard_map(local, mesh=mesh, in_specs=(block, cells, cells, cells), out_specs=block, check_vma=False)
```

```python
import jax
import jax.numpy as jnp
from jax import lax
from jax.experimental import pallas as pl
from jax.experimental.pallas import tpu as pltpu
from jax.sharding import PartitionSpec as P

MESH = pl.DeviceIdType.MESH
F32 = jnp.float32
NX, NY, NZ = 8, 16, 128
LOW, HIGH = 4, 3
EX, EY = NX + LOW + HIGH, 24
X0, X1 = LOW, LOW + NX
Y0, Y1 = LOW, LOW + NY
CARD, RING = 32, 16


def low_y(a):
    return pltpu.roll(a, 1, 1)


def next_y(a):
    return pltpu.roll(a, EY - 1, 1)


def lanes(a):
    return lax.broadcasted_iota(jnp.int32, a.shape, a.ndim - 1)


def low_z(a):
    return jnp.where(lanes(a) == 0, 0.0, pltpu.roll(a, 1, a.ndim - 1))


def next_z(a):
    return jnp.where(lanes(a) == NZ - 1, 0.0, pltpu.roll(a, NZ - 1, a.ndim - 1))


def blocks(start, stop, size):
    count = -(-(stop - start) // size)
    edges = [start + (stop - start) * n // count for n in range(count + 1)]
    return list(zip(edges[:-1], edges[1:]))


def kernel(
    gxn, gyn,
    vel, visc, press, flags, out,
    S, V0, V1, V2, VEL, VI, FL, PR, RAW, RAWIN, VIA, FLA, PRA, VIB, FLB,
    CW, WXY, WXZ, WYZ, EU, EV, DU, DV, DW,
    CARDS, RINGS,
    lsem, xs, xr, ys, yr, gs, gr,
):
    gx, gy = lax.axis_index("gx"), lax.axis_index("gy")
    has_xlo, has_xhi = gx > 0, gx < gxn - 1
    has_ylo, has_yhi = gy > 0, gy < gyn - 1
    xlo, xhi = (gx - 1, gy), (gx + 1, gy)
    ylo, yhi = (gx, gy - 1), (gx, gy + 1)
    px, zh, py = gx // 8, lax.rem(gx // 4, 2), lax.rem(gx, 4)
    zl, core = gy // 2, lax.rem(gy, 2)
    card = (px * 4 + py) * 2 + core
    ring = zh * 8 + zl

    def hops(d, n):
        return min(d, n - d)

    steps = [(dx, dy, dc) for dx in range(4) for dy in range(4) for dc in range(2)]
    steps.sort(key=lambda d: -(hops(d[0], 4) + hops(d[1], 4) + 0.3 * d[2]))
    pxs, pys, cores = [lax.rem(px + d, 4) * 8 for d in range(4)], [lax.rem(py + d, 4) for d in range(4)], (core, 1 - core)
    card_peers = [(pxs[dx] + zh * 4 + pys[dy], zl * 2 + cores[dc]) for dx, dy, dc in steps[:-1]]
    ring_peers = []
    for d in sorted(range(1, RING), key=lambda d: -hops(d, RING)):
        z = lax.rem(ring + d, RING)
        ring_peers.append((px * 8 + (z // 8) * 4 + py, lax.rem(z, 8) * 2 + core))

    own = (pl.ds(X0, NX), pl.ds(Y0, NY))
    local = [
        pltpu.make_async_copy(flags, FL.at[own], lsem.at[0]),
        pltpu.make_async_copy(press, PR.at[pl.ds(1, NX), pl.ds(Y0, NY)], lsem.at[1]),
        pltpu.make_async_copy(vel, VEL, lsem.at[2]),
        pltpu.make_async_copy(visc, VI.at[own], lsem.at[3]),
    ]
    for copy in local:
        copy.start()

    def clear(ref, lead, kind):
        zero = lambda *shape: jnp.zeros(shape, kind)
        for c in range(lead) if lead else [None]:
            at = ref if c is None else ref.at[c]
            at[0:X0] = zero(X0, EY, NZ)
            at[X1:EX] = zero(EX - X1, EY, NZ)
            at[X0:X1, 0:Y0] = zero(NX, Y0, NZ)
            at[X0:X1, Y1:EY] = zero(NX, EY - Y1, NZ)

    clear(S, 3, F32)
    clear(VI, 0, F32)
    clear(FL, 0, jnp.int32)
    PR[0] = jnp.zeros((EY, NZ), F32)
    PR[1:, 0:Y0] = jnp.zeros((NX, Y0, NZ), F32)
    PR[1:, Y1:EY] = jnp.zeros((NX, EY - Y1, NZ), F32)
    RAWIN[...] = jnp.zeros((1, NY, NZ), F32)
    for c in range(3):
        V2[c, X1] = jnp.zeros((EY, NZ), F32)

    barrier = pltpu.get_barrier_semaphore()

    def greet(device):
        pl.semaphore_signal(barrier, inc=1, device_id=device, device_id_type=MESH)

    far_up, far_down = (py == 3) & has_xhi, (py == 0) & has_xlo
    pass_up, pass_down = (py == 2) & (gx < gxn - 2), (py == 1) & (gx >= 2)
    near = [
        (far_up, xhi), (far_down, xlo), (pass_up | far_up, (gx + 2, gy)), (pass_down | far_down, (gx - 2, gy)),
        (has_xlo & (py != 0), xlo), (has_xhi & (py != 3), xhi), (has_ylo, ylo), (has_yhi, yhi),
    ]
    for there, device in near:
        pl.when(there)(lambda device=device: greet(device))

    for device in ring_peers + card_peers:
        greet(device)

    def is_fluid(f):
        return jnp.where(f == 1, 1.0, 0.0)

    def is_open(f):
        return jnp.where(f != 0, 1.0, 0.0)

    def pressed(a, b, y):
        f = FL[a:b, y : y + NY]
        fluid = is_fluid(f)
        return fluid, is_open(f), PR[a - LOW + 1 : b - LOW + 1, y : y + NY] * fluid

    for copy in local[:3]:
        copy.wait()
    for a, b in blocks(X0, X1, 2):
        fluid, opened, p = pressed(a, b, Y0)
        act = jnp.maximum(fluid, low_z(fluid)) * opened * low_z(opened)
        S[2, a:b, Y0:Y1] = act * (VEL[2, a - X0 : b - X0] - (p - low_z(p)))
        if a == X0:
            RAW[...] = VEL[0, 0:1] - p[0:1]
            fluid, opened, p, a = fluid[1:], opened[1:], p[1:], a + 1
        fluid_low, opened_low, p_low = pressed(a - 1, b - 1, Y0)
        act = jnp.maximum(fluid, fluid_low) * opened * opened_low
        S[0, a:b, Y0:Y1] = act * (VEL[0, a - X0 : b - X0] - (p - p_low))

    one = lambda there: jnp.where(there, 1, 0)
    pl.semaphore_wait(barrier, CARD + RING - 2 + sum(one(t) for t, _ in near))

    sent = []

    def send(source, target, sems, n, to, there, from_, out=None):
        copy = pltpu.make_async_remote_copy(
            src_ref=source, dst_ref=target, send_sem=sems[0].at[n if out is None else out], recv_sem=sems[1].at[n],
            device_id=to, device_id_type=MESH,
        )
        pl.when(there)(copy.start)
        sent.append((there, copy))
        return lambda: pl.when(from_)(copy.wait_recv)

    X, Y = (xs, xr), (ys, yr)
    UP, DOWN = (xhi, has_xhi, has_xlo), (xlo, has_xlo, has_xhi)
    NORTH, SOUTH = (yhi, has_yhi, has_ylo), (ylo, has_ylo, has_yhi)
    rows = pl.ds(Y0, NY)
    last4, first3 = pl.ds(NX - LOW, LOW), pl.ds(0, HIGH)
    xlow, xhigh, xown = pl.ds(0, LOW), pl.ds(X1, HIGH), pl.ds(X0, NX)
    ylow, yhigh = pl.ds(0, LOW), pl.ds(Y1, HIGH)
    ylast, yfirst = pl.ds(NY - LOW, LOW), pl.ds(0, HIGH)
    elast, efirst = pl.ds(Y1 - LOW, LOW), pl.ds(Y0, HIGH)

    u, v, w = 0, 1, 2
    upper = pl.ds(X0 + 1, NX - 1)
    top4, low3 = pl.ds(X1 - LOW, LOW), pl.ds(X0, HIGH)
    passing = [
        (visc.at[last4], VIA, VI.at[xlow, rows], 2), (flags.at[last4], FLA, FL.at[xlow, rows], 0),
        (press.at[pl.ds(NX - 1, 1)], PRA, PR.at[pl.ds(0, 1), rows], 4),
    ], [(visc.at[first3], VIB, VI.at[xhigh, rows], 3), (flags.at[first3], FLB, FL.at[xhigh, rows], 1)]
    far_cells = [send(part[0], part[1], X, 14 + k, xlo, far_up, pass_up) for k, part in enumerate(passing[0])]
    far_cells += [send(part[0], part[1], X, 17 + k, xhi, far_down, pass_down) for k, part in enumerate(passing[1])]
    direct_up, direct_down = (xhi, has_xhi & (py != 3), has_xlo), (xlo, has_xlo & (py != 0), has_xhi)
    x_started = [
        send(S.at[u, top4, rows], S.at[u, xlow, rows], X, 5, *UP),
        send(S.at[w, top4, rows], S.at[w, xlow, rows], X, 6, *UP),
        send(RAW, RAWIN, X, 8, *DOWN),
        send(S.at[u, pl.ds(X0 + 1, HIGH - 1), rows], S.at[u, pl.ds(X1 + 1, HIGH - 1), rows], X, 7, *DOWN),
        send(S.at[w, low3, rows], S.at[w, xhigh, rows], X, 11, *DOWN),
    ]
    y_press = send(press.at[:, pl.ds(NY - 1, 1)], PR.at[pl.ds(1, NX), pl.ds(Y0 - 1, 1)], Y, 0, *NORTH)
    y_flags = send(flags.at[:, ylast], FL.at[xown, ylow], Y, 1, *NORTH)
    x_flags = send(flags.at[first3], FL.at[xhigh, rows], X, 1, *direct_down)
    x_visc = send(visc.at[first3], VI.at[xhigh, rows], X, 3, *direct_down)
    x_press = send(press.at[pl.ds(NX - 1, 1)], PR.at[pl.ds(0, 1), rows], X, 4, *direct_up)
    x_cells = [
        send(flags.at[last4], FL.at[xlow, rows], X, 0, *direct_up),
        x_flags,
        send(visc.at[last4], VI.at[xlow, rows], X, 2, *direct_up),
        x_visc,
    ]
    y_cells = [
        send(flags.at[:, yfirst], FL.at[xown, yhigh], Y, 2, *SOUTH),
        send(visc.at[:, ylast], VI.at[xown, ylow], Y, 3, *NORTH),
        send(visc.at[:, yfirst], VI.at[xown, yhigh], Y, 4, *SOUTH),
    ]
    y_started = [
        send(S.at[w, xown, elast], S.at[w, xown, ylow], Y, 5, *NORTH),
        send(S.at[u, upper, elast], S.at[u, upper, ylow], Y, 6, *NORTH),
        send(S.at[w, xown, efirst], S.at[w, xown, yhigh], Y, 7, *SOUTH),
        send(S.at[u, upper, efirst], S.at[u, upper, yhigh], Y, 8, *SOUTH),
    ]

    y_press()
    y_flags()
    for a, b in blocks(X0, X1, 2):
        fluid, opened, p = pressed(a, b, Y0)
        fluid_low, opened_low, p_low = pressed(a, b, Y0 - 1)
        act = jnp.maximum(fluid, fluid_low) * opened * opened_low
        S[1, a:b, Y0:Y1] = act * (VEL[1, a - X0 : b - X0] - (p - p_low))
    x_started += [
        send(S.at[v, top4, rows], S.at[v, xlow, rows], X, 12, *UP),
        send(S.at[v, low3, rows], S.at[v, xhigh, rows], X, 13, *DOWN),
    ]
    y_started += [
        send(S.at[v, xown, elast], S.at[v, xown, ylow], Y, 9, *NORTH),
        send(S.at[v, xown, efirst], S.at[v, xown, yhigh], Y, 10, *SOUTH),
    ]
    for wait in far_cells:
        wait()
    for _, source, target, n in passing[0]:
        send(source, target, X, n, (gx + 2, gy), pass_up, None, out=19 + n)
    for _, source, target, n in passing[1]:
        send(source, target, X, n, (gx - 2, gy), pass_down, None, out=19 + n)

    local[3].wait()
    n = 11
    for wait in x_cells:
        wait()
    for ref in (FL, VI):
        for layers in (xlow, xhigh):
            y_cells.append(send(ref.at[layers, elast], ref.at[layers, ylow], Y, n, *NORTH))
            y_cells.append(send(ref.at[layers, efirst], ref.at[layers, yhigh], Y, n + 1, *SOUTH))
            n += 2
    for wait in y_cells:
        wait()

    for a, b in blocks(1, EX, 5):
        f = is_fluid(FL[a - 1 : b])
        m = VI[a - 1 : b]
        fx, mx = jnp.maximum(f[1:], f[:-1]), m[1:] + m[:-1]
        fc, mc = f[1:], m[1:]
        if a == 1:
            CW[0] = 2.0 * m[0] * f[0]
        CW[a:b] = 2.0 * mc * fc
        WXY[a:b] = 0.25 * (mx + low_y(mx)) * jnp.maximum(fx, low_y(fx))
        WXZ[a:b] = 0.25 * (mx + low_z(mx)) * jnp.maximum(fx, low_z(fx))
        fy, my = jnp.maximum(fc, low_y(fc)), mc + low_y(mc)
        WYZ[a:b] = 0.25 * (my + low_z(my)) * jnp.maximum(fy, low_z(fy))
        top = lanes(fx) == NZ - 1
        EU[a:b] = jnp.where(top, 0.25 * mx * fx, 0.0)
        EV[a:b] = jnp.where(top, 0.25 * my * fy, 0.0)
    for a, b in blocks(1, EX - 1, 5):
        f = FL[a - 1 : b]
        fluid, opened = is_fluid(f), is_open(f)
        fc, oc = fluid[1:], opened[1:]
        cw = CW[a:b]
        wxy, wxz, wyz = WXY[a : b + 1], WXZ[a : b + 1], WYZ[a:b]
        xy, xz = wxy[:-1], wxz[:-1]
        act = jnp.maximum(fc, fluid[:-1]) * oc * opened[:-1]
        DU[a:b] = act / (1.0 + cw + CW[a - 1 : b - 1] + xy + next_y(xy) + xz + next_z(xz) + EU[a:b])
        act = jnp.maximum(fc, low_y(fc)) * oc * low_y(oc)
        DV[a:b] = act / (1.0 + cw + low_y(cw) + xy + wxy[1:] + wyz + next_z(wyz) + EV[a:b])
        act = jnp.maximum(fc, low_z(fc)) * oc * low_z(oc)
        DW[a:b] = act / (1.0 + cw + low_z(cw) + xz + wxz[1:] + wyz + next_y(wyz))

    for wait in x_started:
        wait()
    x_press()
    for layer, below, raw in ((X0, 0, RAW), (X1, NX, RAWIN)):
        f, g = FL[layer : layer + 1, Y0:Y1], FL[layer - 1 : layer, Y0:Y1]
        act = jnp.maximum(is_fluid(f), is_fluid(g)) * is_open(f) * is_open(g)
        S[0, layer : layer + 1, Y0:Y1] = act * (raw[...] + PR[below : below + 1, Y0:Y1] * is_fluid(g))
    lowest = pl.ds(X0, 1)
    for there, at in ((S, (slice(None), xlow)), (S, (slice(None), xhigh)), (S, (0, lowest))):
        y_started.append(send(there.at[(*at, elast)], there.at[(*at, ylow)], Y, n, *NORTH))
        y_started.append(send(there.at[(*at, efirst)], there.at[(*at, yhigh)], Y, n + 1, *SOUTH))
        n += 2
    for wait in y_started:
        wait()

    def gradient(F, a, b):
        u, v, w = F[0, a - 1 : b + 1], F[1, a - 1 : b + 1], F[2, a - 1 : b + 1]
        uc, vc, wc = u[1:-1], v[1:-1], w[1:-1]
        sx = CW[a - 1 : b] * (u[1:] - u[:-1])
        un, vn, wn = u[1:], v[1:], w[1:]
        xy = WXY[a : b + 1] * (un - low_y(un) + vn - v[:-1])
        xz = WXZ[a : b + 1] * (un - low_z(un) + wn - w[:-1])
        cw = CW[a:b]
        sy = cw * (next_y(vc) - vc)
        sz = cw * (next_z(wc) - wc)
        yz = WYZ[a:b] * (vc - low_z(vc) + wc - low_y(wc))
        xyc, xzc = xy[:-1], xz[:-1]
        return (
            sx[:-1] - sx[1:] + xyc - next_y(xyc) + xzc - next_z(xzc) + EU[a:b] * uc,
            low_y(sy) - sy + xyc - xy[1:] + yz - next_z(yz) + EV[a:b] * vc,
            low_z(sz) - sz + xzc - xz[1:] + yz - next_y(yz),
        ), (uc, vc, wc)

    D = (DU, DV, DW)
    row = lax.broadcasted_iota(jnp.int32, (1, EY, NZ), 1)
    inside = (row >= Y0) & (row < Y1)

    def partial(values, a, b, mask):
        lo, hi = max(a, X0), min(b, X1)
        if lo >= hi:
            return jnp.zeros((1, EY, NZ), F32)
        part = values[lo - a : hi - a]
        return jnp.where(mask, jnp.sum(part, axis=0, keepdims=True), 0.0)

    zero = jnp.zeros((1, EY, NZ), F32)
    b0 = h00 = h01 = h11 = h12 = h22 = zero
    for a, b in blocks(1, EX - 1, 4):
        grad, _ = gradient(S, a, b)
        total = 0.0
        for c in range(3):
            z = -D[c][a:b] * grad[c]
            V0[c, a:b] = z
            total = total - z * grad[c]
        b0 = b0 + partial(total, a, b, inside)
    for a, b in blocks(2, EX - 2, 4):
        grad, field = gradient(V0, a, b)
        same = cross = 0.0
        for c in range(3):
            g = field[c] + grad[c]
            z = D[c][a:b] * g - field[c]
            V1[c, a:b] = z
            same, cross = same + field[c] * g, cross + z * g
        h00, h01 = h00 + partial(same, a, b, inside), h01 + partial(cross, a, b, inside)
    for a, b in blocks(3, EX - 3, 4):
        grad, field = gradient(V1, a, b)
        same = cross = 0.0
        for c in range(3):
            g = field[c] + grad[c]
            z = D[c][a:b] * g - field[c]
            V2[c, a:b] = z
            same, cross = same + field[c] * g, cross + z * g
        h11, h12 = h11 + partial(same, a, b, inside), h12 + partial(cross, a, b, inside)
    edge = row == Y1
    upto = inside | (edge & jnp.logical_not(has_yhi))
    below = ((row >= Y0 - 1) & (row < Y1 - 1)) | ((row == Y1 - 1) & jnp.logical_not(has_yhi))
    for a, b in blocks(X0, X1 + 1, 5):
        u, v, w = V2[0, a - 1 : b], V2[1, a - 1 : b], V2[2, a - 1 : b]
        uc, vc, wc = u[1:], v[1:], w[1:]
        cw = CW[a - 1 : b]
        dx = uc - u[:-1]
        xy = uc - low_y(uc) + vc - v[:-1]
        xz = uc - low_z(uc) + wc - w[:-1]
        yz = vc - low_z(vc) + wc - low_y(wc)
        dz = next_z(wc) - wc
        dy = next_y(vc) - vc
        most = (
            cw[:-1] * dx * dx + WXY[a:b] * xy * xy + WXZ[a:b] * xz * xz + WYZ[a:b] * yz * yz
            + cw[1:] * dz * dz + (1.0 + EU[a:b]) * uc * uc + (1.0 + EV[a:b]) * vc * vc + wc * wc
        )
        along = cw[1:] * dy * dy
        value = jnp.where(upto, most, 0.0) + jnp.where(below, along, 0.0)
        h22 = h22 + jnp.sum(value[: min(b, X1) - a], axis=0, keepdims=True)
        if b > X1:
            h22 = h22 + jnp.where(has_xhi, 0.0, value[X1 - a : X1 - a + 1])

    lane = lax.broadcasted_iota(jnp.int32, (1, NZ), 1)
    payload = jnp.zeros((1, NZ), F32)
    for k, value in enumerate((b0, h00, h01, h11, h12, h22)):
        total = jnp.sum(jnp.sum(value[0], axis=0, keepdims=True), axis=1, keepdims=True)
        payload = jnp.where(lane == k, total, payload)

    def gather(slots, me, peers, n, value):
        slots[me] = value
        for device in peers:
            pltpu.make_async_remote_copy(
                src_ref=slots.at[me], dst_ref=slots.at[me], send_sem=gs.at[n], recv_sem=gr.at[n],
                device_id=device, device_id_type=MESH,
            ).start()
        rest = slots.at[pl.ds(0, len(peers))]
        every = pltpu.make_async_remote_copy(
            src_ref=rest, dst_ref=rest, send_sem=gs.at[n], recv_sem=gr.at[n],
            device_id=peers[0], device_id_type=MESH,
        )
        every.wait_recv()
        total = slots[0]
        for r in range(1, len(peers) + 1):
            total = total + slots[r]
        return total, every.wait_send

    total, finish_cards = gather(CARDS, card, card_peers, 0, payload)
    total, finish_rings = gather(RINGS, ring, ring_peers, 1, total)

    wide = jnp.broadcast_to(total, (8, NZ))
    at = lax.broadcasted_iota(jnp.int32, (8, NZ), 1)
    m = [
        jnp.broadcast_to(jnp.sum(jnp.where(at == k, wide, 0.0), axis=1, keepdims=True), (8, NZ))
        for k in range(6)
    ]
    r0, a00, a01, a11, a12, a22 = m
    r1 = a00 - r0
    r2 = a01 - r1
    a02 = a11
    tiny = 1e-6

    def over(top, pivot, size):
        good = pivot > tiny * size
        return jnp.where(good, top / jnp.where(good, pivot, 1.0), 0.0)

    d0 = a00
    l10, l20 = over(a01, d0, 0.0), over(a02, d0, 0.0)
    d1 = a11 - l10 * a01
    e21 = a12 - l20 * a01
    l21 = over(e21, d1, a11)
    d2 = a22 - l20 * a02 - l21 * e21
    y1 = r1 - l10 * r0
    y2 = r2 - l20 * r0 - l21 * y1
    c2 = over(y2, d2, a22)
    c1 = over(y1, d1, a11) - l21 * c2
    c0 = over(r0, d0, 0.0) - l10 * c1 - l20 * c2
    c0, c1, c2 = c0[0:1], c1[0:1], c2[0:1]
    for c in range(3):
        for a, b in blocks(X0, X1, 4):
            out[c, a - X0 : b - X0] = (
                S[c, a:b, Y0:Y1] + c0 * V0[c, a:b, Y0:Y1] + c1 * V1[c, a:b, Y0:Y1] + c2 * V2[c, a:b, Y0:Y1]
            )
    for there, copy in sent:
        pl.when(there)(copy.wait_send)
    finish_cards()
    finish_rings()


def solution(mesh):
    gxn, gyn = mesh.shape["gx"], mesh.shape["gy"]
    block, cells = P(None, "gx", "gy", None), P("gx", "gy", None)
    ext = (EX, EY, NZ)
    field = lambda *shape: pltpu.VMEM(shape, F32)
    dma = lambda n: pltpu.SemaphoreType.DMA((n,))

    def local(velocity, viscosity, pressure, flags):
        def body(*refs):
            kernel(gxn, gyn, *refs)

        return pl.pallas_call(
            body,
            out_shape=jax.ShapeDtypeStruct((3, NX, NY, NZ), F32),
            in_specs=[pl.BlockSpec(memory_space=pl.ANY)] * 4,
            out_specs=pl.BlockSpec(memory_space=pltpu.VMEM),
            scratch_shapes=[
                *[field(3, *ext)] * 4, field(3, NX, NY, NZ), field(*ext), pltpu.VMEM(ext, jnp.int32),
                field(NX + 1, EY, NZ), field(1, NY, NZ), field(1, NY, NZ),
                field(LOW, NY, NZ), pltpu.VMEM((LOW, NY, NZ), jnp.int32), field(1, NY, NZ),
                field(HIGH, NY, NZ), pltpu.VMEM((HIGH, NY, NZ), jnp.int32),
                *[field(*ext)] * 9,
                field(CARD, 1, NZ), field(RING, 1, NZ),
                dma(4), dma(24), dma(19), dma(25), dma(25), dma(2), dma(2),
            ],
            compiler_params=pltpu.CompilerParams(
                collective_id=1, has_side_effects=True, vmem_limit_bytes=48 * 2**20
            ),
        )(*[pltpu.with_memory_space_constraint(a, pltpu.HBM) for a in (velocity, viscosity, pressure, flags)])

    return jax.shard_map(local, mesh=mesh, in_specs=(block, cells, cells, cells), out_specs=block, check_vma=False)
```

```python
import jax
import jax.numpy as jnp
from jax import lax
from jax.experimental import pallas as pl
from jax.experimental.pallas import tpu as pltpu
from jax.sharding import PartitionSpec as P

MESH = pl.DeviceIdType.MESH
F32 = jnp.float32
NX, NY, NZ = 8, 16, 128
LOW, HIGH = 4, 3
EX, EY = NX + LOW + HIGH, 24
X0, X1 = LOW, LOW + NX
Y0, Y1 = LOW, LOW + NY
CARD, RING = 32, 16


def low_y(a):
    return pltpu.roll(a, 1, 1)


def next_y(a):
    return pltpu.roll(a, EY - 1, 1)


def lanes(a):
    return lax.broadcasted_iota(jnp.int32, a.shape, a.ndim - 1)


def low_z(a):
    return jnp.where(lanes(a) == 0, 0.0, pltpu.roll(a, 1, a.ndim - 1))


def next_z(a):
    return jnp.where(lanes(a) == NZ - 1, 0.0, pltpu.roll(a, NZ - 1, a.ndim - 1))


def blocks(start, stop, size):
    count = -(-(stop - start) // size)
    edges = [start + (stop - start) * n // count for n in range(count + 1)]
    return list(zip(edges[:-1], edges[1:]))


def kernel(
    gxn, gyn,
    vel, visc, press, flags, out,
    S, V0, V1, V2, VEL, VI, FL, PR, RAW, RAWIN, VIA, FLA, VIB,
    CW, WXY, WXZ, WYZ, EU, EV, DU, DV, DW,
    CARDS, RINGS,
    lsem, xs, xr, ys, yr, gs, gr,
):
    gx, gy = lax.axis_index("gx"), lax.axis_index("gy")
    has_xlo, has_xhi = gx > 0, gx < gxn - 1
    has_ylo, has_yhi = gy > 0, gy < gyn - 1
    xlo, xhi = (gx - 1, gy), (gx + 1, gy)
    ylo, yhi = (gx, gy - 1), (gx, gy + 1)
    px, zh, py = gx // 8, lax.rem(gx // 4, 2), lax.rem(gx, 4)
    zl, core = gy // 2, lax.rem(gy, 2)
    card = (px * 4 + py) * 2 + core
    ring = zh * 8 + zl

    def hops(d, n):
        return min(d, n - d)

    steps = [(dx, dy, dc) for dx in range(4) for dy in range(4) for dc in range(2)]
    steps.sort(key=lambda d: -(hops(d[0], 4) + hops(d[1], 4) + 0.3 * d[2]))
    pxs, pys, cores = [lax.rem(px + d, 4) * 8 for d in range(4)], [lax.rem(py + d, 4) for d in range(4)], (core, 1 - core)
    card_peers = [(pxs[dx] + zh * 4 + pys[dy], zl * 2 + cores[dc]) for dx, dy, dc in steps[:-1]]
    ring_peers = []
    for d in sorted(range(1, RING), key=lambda d: -hops(d, RING)):
        z = lax.rem(ring + d, RING)
        ring_peers.append((px * 8 + (z // 8) * 4 + py, lax.rem(z, 8) * 2 + core))

    own = (pl.ds(X0, NX), pl.ds(Y0, NY))
    local = [
        pltpu.make_async_copy(flags, FL.at[own], lsem.at[0]),
        pltpu.make_async_copy(press, PR.at[pl.ds(1, NX), pl.ds(Y0, NY)], lsem.at[1]),
        pltpu.make_async_copy(vel, VEL, lsem.at[2]),
        pltpu.make_async_copy(visc, VI.at[own], lsem.at[3]),
    ]
    for copy in local:
        copy.start()

    @pl.when((gx == 0) | (gx == gxn - 1) | (gy == 0) | (gy == gyn - 1))
    def _():
        for ref in (S.at[0], S.at[1], S.at[2], VI, FL):
            ref[0:X0] = jnp.zeros((X0, EY, NZ), ref.dtype)
            ref[X1:EX] = jnp.zeros((EX - X1, EY, NZ), ref.dtype)
            ref[X0:X1, 0:Y0] = jnp.zeros((NX, Y0, NZ), ref.dtype)
            ref[X0:X1, Y1:EY] = jnp.zeros((NX, EY - Y1, NZ), ref.dtype)
        PR[0] = jnp.zeros((EY, NZ), F32)
        PR[1:, 0:Y0] = jnp.zeros((NX, Y0, NZ), F32)
        RAWIN[...] = jnp.zeros((1, NY, NZ), F32)
        for c in range(3):
            V2[c, X1] = jnp.zeros((EY, NZ), F32)

    barrier = pltpu.get_barrier_semaphore()

    def greet(device):
        pl.semaphore_signal(barrier, inc=1, device_id=device, device_id_type=MESH)

    far_up, far_down = (py == 3) & has_xhi, (py == 0) & has_xlo
    pass_up, pass_down = (py == 2) & (gx < gxn - 2), (py == 1) & (gx >= 2)
    near = [
        (far_up, xhi), (far_down, xlo), (pass_up | far_up, (gx + 2, gy)), (pass_down | far_down, (gx - 2, gy)),
        (has_xlo & (py != 0), xlo), (has_xhi & (py != 3), xhi), (has_ylo, ylo), (has_yhi, yhi),
    ]
    for there, device in near:
        pl.when(there)(lambda device=device: greet(device))

    for device in ring_peers + card_peers:
        greet(device)

    def is_fluid(f):
        return jnp.where(f == 1, 1.0, 0.0)

    def is_open(f):
        return jnp.where(f != 0, 1.0, 0.0)

    def pressed(a, b, y):
        f = FL[a:b, y : y + NY]
        fluid = is_fluid(f)
        return fluid, is_open(f), PR[a - LOW + 1 : b - LOW + 1, y : y + NY] * fluid

    for copy in local[:3]:
        copy.wait()
    for a, b in blocks(X0, X1, 2):
        fluid, opened, p = pressed(a, b, Y0)
        act = jnp.maximum(fluid, low_z(fluid)) * opened * low_z(opened)
        S[2, a:b, Y0:Y1] = act * (VEL[2, a - X0 : b - X0] - (p - low_z(p)))
        if a == X0:
            RAW[...] = VEL[0, 0:1] - p[0:1]
            fluid, opened, p, a = fluid[1:], opened[1:], p[1:], a + 1
        fluid_low, opened_low, p_low = pressed(a - 1, b - 1, Y0)
        act = jnp.maximum(fluid, fluid_low) * opened * opened_low
        S[0, a:b, Y0:Y1] = act * (VEL[0, a - X0 : b - X0] - (p - p_low))

    one = lambda there: jnp.where(there, 1, 0)
    pl.semaphore_wait(barrier, CARD + RING - 2 + sum(one(t) for t, _ in near))

    sent = []

    def send(source, target, sems, n, to, there, from_, out=None, later=None):
        copy = pltpu.make_async_remote_copy(
            src_ref=source, dst_ref=target, send_sem=sems[0].at[n if out is None else out], recv_sem=sems[1].at[n],
            device_id=to, device_id_type=MESH,
        )
        if later is None:
            pl.when(there)(copy.start)
        else:
            later.append((there, copy))
        sent.append((there, copy))
        return lambda: pl.when(from_)(copy.wait_recv)

    X, Y = (xs, xr), (ys, yr)
    UP, DOWN = (xhi, has_xhi, has_xlo), (xlo, has_xlo, has_xhi)
    NORTH, SOUTH = (yhi, has_yhi, has_ylo), (ylo, has_ylo, has_yhi)
    rows = pl.ds(Y0, NY)
    last4, first3 = pl.ds(NX - LOW, LOW), pl.ds(0, HIGH)
    xlow, xhigh, xown = pl.ds(0, LOW), pl.ds(X1, HIGH), pl.ds(X0, NX)
    ylow, yhigh = pl.ds(0, LOW), pl.ds(Y1, HIGH)
    ylast, yfirst = pl.ds(NY - LOW, LOW), pl.ds(0, HIGH)
    elast, efirst = pl.ds(Y1 - LOW, LOW), pl.ds(Y0, HIGH)

    def start(up, down, far):
        for copies, crosses in ((up, py == 3), (down, py == 0)):
            for there, copy in copies:
                pl.when(there & (crosses if far else jnp.logical_not(crosses)))(copy.start)

    up, down = [], []
    y_press = send(press.at[:, pl.ds(NY - 1, 1)], PR.at[pl.ds(1, NX), pl.ds(Y0 - 1, 1)], Y, 0, *NORTH)
    y_flags = send(flags.at[:, ylast], FL.at[xown, ylow], Y, 1, *NORTH)
    u, v, w = 0, 1, 2
    upper = pl.ds(X0 + 1, NX - 1)
    top4, low3 = pl.ds(X1 - LOW, LOW), pl.ds(X0, HIGH)
    half = LOW // 2
    passing = [
        (visc.at[last4], VIA, VI.at[xlow, rows], 2),
        (flags.at[pl.ds(NX - LOW, half)], FLA, FL.at[pl.ds(0, half), rows], 0),
    ], [(visc.at[first3], VIB, VI.at[xhigh, rows], 3)]
    far_cells = [send(part[0], part[1], X, 14 + k, xlo, far_up, pass_up) for k, part in enumerate(passing[0])]
    far_cells += [send(part[0], part[1], X, 17 + k, xhi, far_down, pass_down) for k, part in enumerate(passing[1])]
    direct_up, direct_down = (xhi, has_xhi & (py != 3), has_xlo), (xlo, has_xlo & (py != 0), has_xhi)
    x_started = [
        send(S.at[u, top4, rows], S.at[u, xlow, rows], X, 5, *UP, later=up),
        send(S.at[w, top4, rows], S.at[w, xlow, rows], X, 6, *UP, later=up),
        send(RAW, RAWIN, X, 8, *DOWN, later=down),
        send(S.at[u, pl.ds(X0 + 1, HIGH - 1), rows], S.at[u, pl.ds(X1 + 1, HIGH - 1), rows], X, 7, *DOWN, later=down),
        send(S.at[w, low3, rows], S.at[w, xhigh, rows], X, 11, *DOWN, later=down),
    ]
    x_cells = [
        send(flags.at[first3], FL.at[xhigh, rows], X, 1, *DOWN, later=down),
        send(flags.at[pl.ds(NX - half, half)], FL.at[pl.ds(half, half), rows], X, 16, *UP, later=up),
    ]
    x_press = send(press.at[pl.ds(NX - 1, 1)], PR.at[pl.ds(0, 1), rows], X, 4, *UP, later=up)
    start(up, down, True)
    x_cells += [
        send(flags.at[pl.ds(NX - LOW, half)], FL.at[pl.ds(0, half), rows], X, 0, *direct_up, later=up),
        send(visc.at[last4], VI.at[xlow, rows], X, 2, *direct_up, later=up),
        send(visc.at[first3], VI.at[xhigh, rows], X, 3, *direct_down, later=down),
    ]
    near_up, near_down = up, down
    up, down = [], []
    y_cells = [
        send(flags.at[:, yfirst], FL.at[xown, yhigh], Y, 2, *SOUTH),
        send(visc.at[:, ylast], VI.at[xown, ylow], Y, 3, *NORTH),
        send(visc.at[:, yfirst], VI.at[xown, yhigh], Y, 4, *SOUTH),
    ]
    y_started = [
        send(S.at[w, xown, elast], S.at[w, xown, ylow], Y, 5, *NORTH),
        send(S.at[u, upper, elast], S.at[u, upper, ylow], Y, 6, *NORTH),
        send(S.at[w, xown, efirst], S.at[w, xown, yhigh], Y, 7, *SOUTH),
        send(S.at[u, upper, efirst], S.at[u, upper, yhigh], Y, 8, *SOUTH),
    ]

    y_press()
    y_flags()
    for a, b in blocks(X0, X1, 2):
        fluid, opened, p = pressed(a, b, Y0)
        fluid_low, opened_low, p_low = pressed(a, b, Y0 - 1)
        act = jnp.maximum(fluid, fluid_low) * opened * opened_low
        S[1, a:b, Y0:Y1] = act * (VEL[1, a - X0 : b - X0] - (p - p_low))
    x_started += [
        send(S.at[v, top4, rows], S.at[v, xlow, rows], X, 12, *UP, later=up),
        send(S.at[v, low3, rows], S.at[v, xhigh, rows], X, 13, *DOWN, later=down),
    ]
    start(up, down, True)
    y_started += [
        send(S.at[v, xown, elast], S.at[v, xown, ylow], Y, 9, *NORTH),
        send(S.at[v, xown, efirst], S.at[v, xown, yhigh], Y, 10, *SOUTH),
    ]
    for wait in far_cells:
        wait()
    for _, source, target, n in passing[0]:
        send(source, target, X, n, (gx + 2, gy), pass_up, None, out=19 + n)
    for _, source, target, n in passing[1]:
        send(source, target, X, n, (gx - 2, gy), pass_down, None, out=19 + n)
    start(near_up + up, near_down + down, False)

    local[3].wait()
    n = 11
    for wait in x_cells:
        wait()
    for ref in (FL, VI):
        for layers in (xlow, xhigh):
            y_cells.append(send(ref.at[layers, elast], ref.at[layers, ylow], Y, n, *NORTH))
            y_cells.append(send(ref.at[layers, efirst], ref.at[layers, yhigh], Y, n + 1, *SOUTH))
            n += 2
    for wait in x_started:
        wait()
    x_press()
    for layer, below, raw in ((X0, 0, RAW), (X1, NX, RAWIN)):
        f, g = FL[layer : layer + 1, Y0:Y1], FL[layer - 1 : layer, Y0:Y1]
        act = jnp.maximum(is_fluid(f), is_fluid(g)) * is_open(f) * is_open(g)
        S[0, layer : layer + 1, Y0:Y1] = act * (raw[...] + PR[below : below + 1, Y0:Y1] * is_fluid(g))
    lowest = pl.ds(X0, 1)
    for there, at in ((S, (slice(None), xlow)), (S, (slice(None), xhigh)), (S, (0, lowest))):
        y_started.append(send(there.at[(*at, elast)], there.at[(*at, ylow)], Y, n, *NORTH))
        y_started.append(send(there.at[(*at, efirst)], there.at[(*at, yhigh)], Y, n + 1, *SOUTH))
        n += 2
    for wait in y_cells:
        wait()

    for a, b in blocks(1, EX, 5):
        f = is_fluid(FL[a - 1 : b])
        m = VI[a - 1 : b]
        fx, mx = jnp.maximum(f[1:], f[:-1]), m[1:] + m[:-1]
        fc, mc = f[1:], m[1:]
        if a == 1:
            CW[0] = 2.0 * m[0] * f[0]
        CW[a:b] = 2.0 * mc * fc
        WXY[a:b] = 0.25 * (mx + low_y(mx)) * jnp.maximum(fx, low_y(fx))
        WXZ[a:b] = 0.25 * (mx + low_z(mx)) * jnp.maximum(fx, low_z(fx))
        fy, my = jnp.maximum(fc, low_y(fc)), mc + low_y(mc)
        WYZ[a:b] = 0.25 * (my + low_z(my)) * jnp.maximum(fy, low_z(fy))
        top = lanes(fx) == NZ - 1
        EU[a:b] = jnp.where(top, 0.25 * mx * fx, 0.0)
        EV[a:b] = jnp.where(top, 0.25 * my * fy, 0.0)
    for a, b in blocks(1, EX - 1, 5):
        f = FL[a - 1 : b]
        fluid, opened = is_fluid(f), is_open(f)
        fc, oc = fluid[1:], opened[1:]
        cw = CW[a:b]
        wxy, wxz, wyz = WXY[a : b + 1], WXZ[a : b + 1], WYZ[a:b]
        xy, xz = wxy[:-1], wxz[:-1]
        act = jnp.maximum(fc, fluid[:-1]) * oc * opened[:-1]
        DU[a:b] = act / (1.0 + cw + CW[a - 1 : b - 1] + xy + next_y(xy) + xz + next_z(xz) + EU[a:b])
        act = jnp.maximum(fc, low_y(fc)) * oc * low_y(oc)
        DV[a:b] = act / (1.0 + cw + low_y(cw) + xy + wxy[1:] + wyz + next_z(wyz) + EV[a:b])
        act = jnp.maximum(fc, low_z(fc)) * oc * low_z(oc)
        DW[a:b] = act / (1.0 + cw + low_z(cw) + xz + wxz[1:] + wyz + next_y(wyz))

    for wait in y_started:
        wait()

    def gradient(F, a, b):
        u, v, w = F[0, a - 1 : b + 1], F[1, a - 1 : b + 1], F[2, a - 1 : b + 1]
        uc, vc, wc = u[1:-1], v[1:-1], w[1:-1]
        sx = CW[a - 1 : b] * (u[1:] - u[:-1])
        un, vn, wn = u[1:], v[1:], w[1:]
        xy = WXY[a : b + 1] * (un - low_y(un) + vn - v[:-1])
        xz = WXZ[a : b + 1] * (un - low_z(un) + wn - w[:-1])
        cw = CW[a:b]
        sy = cw * (next_y(vc) - vc)
        sz = cw * (next_z(wc) - wc)
        yz = WYZ[a:b] * (vc - low_z(vc) + wc - low_y(wc))
        xyc, xzc = xy[:-1], xz[:-1]
        return (
            sx[:-1] - sx[1:] + xyc - next_y(xyc) + xzc - next_z(xzc) + EU[a:b] * uc,
            low_y(sy) - sy + xyc - xy[1:] + yz - next_z(yz) + EV[a:b] * vc,
            low_z(sz) - sz + xzc - xz[1:] + yz - next_y(yz),
        ), (uc, vc, wc)

    D = (DU, DV, DW)
    row = lax.broadcasted_iota(jnp.int32, (1, EY, NZ), 1)
    inside = (row >= Y0) & (row < Y1)

    def partial(values, a, b, mask):
        lo, hi = max(a, X0), min(b, X1)
        if lo >= hi:
            return jnp.zeros((1, EY, NZ), F32)
        part = values[lo - a : hi - a]
        return jnp.where(mask, jnp.sum(part, axis=0, keepdims=True), 0.0)

    zero = jnp.zeros((1, EY, NZ), F32)
    b0 = h00 = h01 = h11 = h12 = h22 = zero
    for a, b in blocks(1, EX - 1, 4):
        grad, _ = gradient(S, a, b)
        total = 0.0
        for c in range(3):
            z = -D[c][a:b] * grad[c]
            V0[c, a:b] = z
            total = total - z * grad[c]
        b0 = b0 + partial(total, a, b, inside)
    for a, b in blocks(2, EX - 2, 4):
        grad, field = gradient(V0, a, b)
        same = cross = 0.0
        for c in range(3):
            g = field[c] + grad[c]
            z = D[c][a:b] * g - field[c]
            V1[c, a:b] = z
            same, cross = same + field[c] * g, cross + z * g
        h00, h01 = h00 + partial(same, a, b, inside), h01 + partial(cross, a, b, inside)
    for a, b in blocks(3, EX - 3, 4):
        grad, field = gradient(V1, a, b)
        same = cross = 0.0
        for c in range(3):
            g = field[c] + grad[c]
            z = D[c][a:b] * g - field[c]
            V2[c, a:b] = z
            same, cross = same + field[c] * g, cross + z * g
        h11, h12 = h11 + partial(same, a, b, inside), h12 + partial(cross, a, b, inside)
    edge = row == Y1
    upto = inside | (edge & jnp.logical_not(has_yhi))
    below = ((row >= Y0 - 1) & (row < Y1 - 1)) | ((row == Y1 - 1) & jnp.logical_not(has_yhi))
    for a, b in blocks(X0, X1 + 1, 5):
        u, v, w = V2[0, a - 1 : b], V2[1, a - 1 : b], V2[2, a - 1 : b]
        uc, vc, wc = u[1:], v[1:], w[1:]
        cw = CW[a - 1 : b]
        dx = uc - u[:-1]
        xy = uc - low_y(uc) + vc - v[:-1]
        xz = uc - low_z(uc) + wc - w[:-1]
        yz = vc - low_z(vc) + wc - low_y(wc)
        dz = next_z(wc) - wc
        dy = next_y(vc) - vc
        most = (
            cw[:-1] * dx * dx + WXY[a:b] * xy * xy + WXZ[a:b] * xz * xz + WYZ[a:b] * yz * yz
            + cw[1:] * dz * dz + (1.0 + EU[a:b]) * uc * uc + (1.0 + EV[a:b]) * vc * vc + wc * wc
        )
        along = cw[1:] * dy * dy
        value = jnp.where(upto, most, 0.0) + jnp.where(below, along, 0.0)
        h22 = h22 + jnp.sum(value[: min(b, X1) - a], axis=0, keepdims=True)
        if b > X1:
            h22 = h22 + jnp.where(has_xhi, 0.0, value[X1 - a : X1 - a + 1])

    lane = lax.broadcasted_iota(jnp.int32, (1, NZ), 1)
    payload = jnp.zeros((1, NZ), F32)
    for k, value in enumerate((b0, h00, h01, h11, h12, h22)):
        total = jnp.sum(jnp.sum(value[0], axis=0, keepdims=True), axis=1, keepdims=True)
        payload = jnp.where(lane == k, total, payload)

    def gather(slots, me, peers, n, value, meanwhile):
        slots[me] = value
        for device in peers:
            pltpu.make_async_remote_copy(
                src_ref=slots.at[me], dst_ref=slots.at[me], send_sem=gs.at[n], recv_sem=gr.at[n],
                device_id=device, device_id_type=MESH,
            ).start()
        rest = slots.at[pl.ds(0, len(peers))]
        every = pltpu.make_async_remote_copy(
            src_ref=rest, dst_ref=rest, send_sem=gs.at[n], recv_sem=gr.at[n],
            device_id=peers[0], device_id_type=MESH,
        )
        meanwhile()
        every.wait_recv()
        total = slots[0]
        for r in range(1, len(peers) + 1):
            total = total + slots[r]
        return total, every.wait_send

    def finish_sent():
        for there, copy in sent:
            pl.when(there)(copy.wait_send)

    total, finish_cards = gather(CARDS, card, card_peers, 0, payload, finish_sent)
    total, finish_rings = gather(RINGS, ring, ring_peers, 1, total, finish_cards)

    wide = jnp.broadcast_to(total, (8, NZ))
    at = lax.broadcasted_iota(jnp.int32, (8, NZ), 1)
    m = [
        jnp.broadcast_to(jnp.sum(jnp.where(at == k, wide, 0.0), axis=1, keepdims=True), (8, NZ))
        for k in range(6)
    ]
    r0, a00, a01, a11, a12, a22 = m
    r1 = a00 - r0
    r2 = a01 - r1
    a02 = a11
    tiny = 1e-6

    def over(top, pivot, size):
        good = pivot > tiny * size
        return jnp.where(good, top / jnp.where(good, pivot, 1.0), 0.0)

    d0 = a00
    l10, l20 = over(a01, d0, 0.0), over(a02, d0, 0.0)
    d1 = a11 - l10 * a01
    e21 = a12 - l20 * a01
    l21 = over(e21, d1, a11)
    d2 = a22 - l20 * a02 - l21 * e21
    y1 = r1 - l10 * r0
    y2 = r2 - l20 * r0 - l21 * y1
    c2 = over(y2, d2, a22)
    c1 = over(y1, d1, a11) - l21 * c2
    c0 = over(r0, d0, 0.0) - l10 * c1 - l20 * c2
    c0, c1, c2 = c0[0:1], c1[0:1], c2[0:1]
    for c in range(3):
        for a, b in blocks(X0, X1, 4):
            out[c, a - X0 : b - X0] = (
                S[c, a:b, Y0:Y1] + c0 * V0[c, a:b, Y0:Y1] + c1 * V1[c, a:b, Y0:Y1] + c2 * V2[c, a:b, Y0:Y1]
            )
    finish_rings()


def solution(mesh):
    gxn, gyn = mesh.shape["gx"], mesh.shape["gy"]
    block, cells = P(None, "gx", "gy", None), P("gx", "gy", None)
    ext = (EX, EY, NZ)
    field = lambda *shape: pltpu.VMEM(shape, F32)
    dma = lambda n: pltpu.SemaphoreType.DMA((n,))

    def local(velocity, viscosity, pressure, flags):
        def body(*refs):
            kernel(gxn, gyn, *refs)

        return pl.pallas_call(
            body,
            out_shape=jax.ShapeDtypeStruct((3, NX, NY, NZ), F32),
            in_specs=[pl.BlockSpec(memory_space=pl.ANY)] * 4,
            out_specs=pl.BlockSpec(memory_space=pltpu.VMEM),
            scratch_shapes=[
                *[field(3, *ext)] * 4, field(3, NX, NY, NZ), field(*ext), pltpu.VMEM(ext, jnp.int32),
                field(NX + 1, EY, NZ), field(1, NY, NZ), field(1, NY, NZ),
                field(LOW, NY, NZ), pltpu.VMEM((LOW // 2, NY, NZ), jnp.int32), field(HIGH, NY, NZ),
                *[field(*ext)] * 9,
                field(CARD, 1, NZ), field(RING, 1, NZ),
                dma(4), dma(24), dma(19), dma(25), dma(25), dma(2), dma(2),
            ],
            compiler_params=pltpu.CompilerParams(
                collective_id=1, has_side_effects=True, vmem_limit_bytes=48 * 2**20
            ),
        )(*[pltpu.with_memory_space_constraint(a, pltpu.HBM) for a in (velocity, viscosity, pressure, flags)])

    return jax.shard_map(local, mesh=mesh, in_specs=(block, cells, cells, cells), out_specs=block, check_vma=False)
```

```python
import jax
import jax.numpy as jnp
from jax import lax
from jax.experimental import pallas as pl
from jax.experimental.pallas import tpu as pltpu
from jax.sharding import PartitionSpec as P

MESH = pl.DeviceIdType.MESH
F32 = jnp.float32
NX, NY, NZ = 8, 16, 128
LOW, HIGH = 4, 3
EX, EY = NX + LOW + HIGH, 24
X0, X1 = LOW, LOW + NX
Y0, Y1 = LOW, LOW + NY
CARD, RING = 32, 16


def low_y(a):
    return pltpu.roll(a, 1, 1)


def next_y(a):
    return pltpu.roll(a, EY - 1, 1)


def lanes(a):
    return lax.broadcasted_iota(jnp.int32, a.shape, a.ndim - 1)


def low_z(a):
    return jnp.where(lanes(a) == 0, 0.0, pltpu.roll(a, 1, a.ndim - 1))


def next_z(a):
    return jnp.where(lanes(a) == NZ - 1, 0.0, pltpu.roll(a, NZ - 1, a.ndim - 1))


def blocks(start, stop, size):
    count = -(-(stop - start) // size)
    edges = [start + (stop - start) * n // count for n in range(count + 1)]
    return list(zip(edges[:-1], edges[1:]))


def kernel(
    gxn, gyn,
    vel, visc, press, flags, out,
    S, V0, V1, V2, VEL, VI, FL, PR, RAW, RAWIN, VIA, FLA, VIB, FLB, PRA,
    CW, WXY, WXZ, WYZ, EU, EV, DU, DV, DW,
    CARDS, RINGS,
    lsem, xs, xr, ys, yr, gs, gr,
):
    gx, gy = lax.axis_index("gx"), lax.axis_index("gy")
    has_xlo, has_xhi = gx > 0, gx < gxn - 1
    has_ylo, has_yhi = gy > 0, gy < gyn - 1
    xlo, xhi = (gx - 1, gy), (gx + 1, gy)
    ylo, yhi = (gx, gy - 1), (gx, gy + 1)
    px, zh, py = gx // 8, lax.rem(gx // 4, 2), lax.rem(gx, 4)
    zl, core = gy // 2, lax.rem(gy, 2)
    card = (px * 4 + py) * 2 + core
    ring = zh * 8 + zl

    def hops(d, n):
        return min(d, n - d)

    steps = [(dx, dy, dc) for dx in range(4) for dy in range(4) for dc in range(2)]
    steps.sort(key=lambda d: -(hops(d[0], 4) + hops(d[1], 4) + 0.3 * d[2]))
    pxs, pys, cores = [lax.rem(px + d, 4) * 8 for d in range(4)], [lax.rem(py + d, 4) for d in range(4)], (core, 1 - core)
    card_peers = [(pxs[dx] + zh * 4 + pys[dy], zl * 2 + cores[dc]) for dx, dy, dc in steps[:-1]]
    ring_peers = []
    for d in sorted(range(1, RING), key=lambda d: -hops(d, RING)):
        z = lax.rem(ring + d, RING)
        ring_peers.append((px * 8 + (z // 8) * 4 + py, lax.rem(z, 8) * 2 + core))

    own = (pl.ds(X0, NX), pl.ds(Y0, NY))
    local = [
        pltpu.make_async_copy(flags, FL.at[own], lsem.at[0]),
        pltpu.make_async_copy(press, PR.at[pl.ds(1, NX), pl.ds(Y0, NY)], lsem.at[1]),
        pltpu.make_async_copy(vel, VEL, lsem.at[2]),
        pltpu.make_async_copy(visc, VI.at[own], lsem.at[3]),
    ]
    for copy in local:
        copy.start()

    @pl.when((gx == 0) | (gx == gxn - 1) | (gy == 0) | (gy == gyn - 1))
    def _():
        for ref in (S.at[0], S.at[1], S.at[2], VI, FL):
            ref[0:X0] = jnp.zeros((X0, EY, NZ), ref.dtype)
            ref[X1:EX] = jnp.zeros((EX - X1, EY, NZ), ref.dtype)
            ref[X0:X1, 0:Y0] = jnp.zeros((NX, Y0, NZ), ref.dtype)
            ref[X0:X1, Y1:EY] = jnp.zeros((NX, EY - Y1, NZ), ref.dtype)
        PR[0] = jnp.zeros((EY, NZ), F32)
        PR[1:, 0:Y0] = jnp.zeros((NX, Y0, NZ), F32)
        RAWIN[...] = jnp.zeros((1, NY, NZ), F32)
        for c in range(3):
            V2[c, X1] = jnp.zeros((EY, NZ), F32)

    barrier = pltpu.get_barrier_semaphore()

    def greet(device):
        pl.semaphore_signal(barrier, inc=1, device_id=device, device_id_type=MESH)

    far_up, far_down = (py == 3) & has_xhi, (py == 0) & has_xlo
    pass_up, pass_down = (py == 2) & (gx < gxn - 2), (py == 1) & (gx >= 2)
    near = [
        (far_up, xhi), (far_down, xlo), (pass_up | far_up, (gx + 2, gy)), (pass_down | far_down, (gx - 2, gy)),
        (has_xlo & (py != 0), xlo), (has_xhi & (py != 3), xhi), (has_ylo, ylo), (has_yhi, yhi),
    ]
    for there, device in near:
        pl.when(there)(lambda device=device: greet(device))

    for device in ring_peers + card_peers:
        greet(device)

    def is_fluid(f):
        return jnp.where(f == 1, 1.0, 0.0)

    def is_open(f):
        return jnp.where(f != 0, 1.0, 0.0)

    def pressed(a, b, y):
        f = FL[a:b, y : y + NY]
        fluid = is_fluid(f)
        return fluid, is_open(f), PR[a - LOW + 1 : b - LOW + 1, y : y + NY] * fluid

    for copy in local[:3]:
        copy.wait()
    for a, b in blocks(X0, X1, 2):
        fluid, opened, p = pressed(a, b, Y0)
        act = jnp.maximum(fluid, low_z(fluid)) * opened * low_z(opened)
        S[2, a:b, Y0:Y1] = act * (VEL[2, a - X0 : b - X0] - (p - low_z(p)))
        if a == X0:
            RAW[...] = VEL[0, 0:1] - p[0:1]
            fluid, opened, p, a = fluid[1:], opened[1:], p[1:], a + 1
        fluid_low, opened_low, p_low = pressed(a - 1, b - 1, Y0)
        act = jnp.maximum(fluid, fluid_low) * opened * opened_low
        S[0, a:b, Y0:Y1] = act * (VEL[0, a - X0 : b - X0] - (p - p_low))

    one = lambda there: jnp.where(there, 1, 0)
    pl.semaphore_wait(barrier, CARD + RING - 2 + sum(one(t) for t, _ in near))

    sent = []

    def send(source, target, sems, n, to, there, from_, out=None, later=None):
        copy = pltpu.make_async_remote_copy(
            src_ref=source, dst_ref=target, send_sem=sems[0].at[n if out is None else out], recv_sem=sems[1].at[n],
            device_id=to, device_id_type=MESH,
        )
        if later is None:
            pl.when(there)(copy.start)
        else:
            later.append((there, copy))
        sent.append((there, copy))
        return lambda: pl.when(from_)(copy.wait_recv)

    X, Y = (xs, xr), (ys, yr)
    UP, DOWN = (xhi, has_xhi, has_xlo), (xlo, has_xlo, has_xhi)
    NORTH, SOUTH = (yhi, has_yhi, has_ylo), (ylo, has_ylo, has_yhi)
    rows = pl.ds(Y0, NY)
    last4, first3 = pl.ds(NX - LOW, LOW), pl.ds(0, HIGH)
    xlow, xhigh, xown = pl.ds(0, LOW), pl.ds(X1, HIGH), pl.ds(X0, NX)
    ylow, yhigh = pl.ds(0, LOW), pl.ds(Y1, HIGH)
    ylast, yfirst = pl.ds(NY - LOW, LOW), pl.ds(0, HIGH)
    elast, efirst = pl.ds(Y1 - LOW, LOW), pl.ds(Y0, HIGH)

    def start(up, down, far):
        for copies, crosses in ((up, py == 3), (down, py == 0)):
            for there, copy in copies:
                pl.when(there & (crosses if far else jnp.logical_not(crosses)))(copy.start)

    up, down = [], []
    y_press = send(press.at[:, pl.ds(NY - 1, 1)], PR.at[pl.ds(1, NX), pl.ds(Y0 - 1, 1)], Y, 0, *NORTH)
    y_flags = send(flags.at[:, ylast], FL.at[xown, ylow], Y, 1, *NORTH)
    u, v, w = 0, 1, 2
    upper = pl.ds(X0 + 1, NX - 1)
    top4, low3 = pl.ds(X1 - LOW, LOW), pl.ds(X0, HIGH)
    passing = [
        (flags.at[last4], FLA, FL.at[xlow, rows], 0),
        (visc.at[last4], VIA, VI.at[xlow, rows], 2),
    ], [
        (flags.at[first3], FLB, FL.at[xhigh, rows], 1),
        (visc.at[first3], VIB, VI.at[xhigh, rows], 3),
    ]
    far_cells = [send(part[0], part[1], X, (9, 10, 14)[k], xlo, far_up, pass_up) for k, part in enumerate(passing[0])]
    far_cells += [send(part[0], part[1], X, 17 + k, xhi, far_down, pass_down) for k, part in enumerate(passing[1])]
    direct_up, direct_down = (xhi, has_xhi & (py != 3), has_xlo), (xlo, has_xlo & (py != 0), has_xhi)
    x_started = [
        send(S.at[u, top4, rows], S.at[u, xlow, rows], X, 5, *UP, later=up),
        send(S.at[w, top4, rows], S.at[w, xlow, rows], X, 6, *UP, later=up),
        send(RAW, RAWIN, X, 8, *DOWN, later=down),
        send(S.at[u, pl.ds(X0 + 1, HIGH - 1), rows], S.at[u, pl.ds(X1 + 1, HIGH - 1), rows], X, 7, *DOWN, later=down),
        send(S.at[w, low3, rows], S.at[w, xhigh, rows], X, 11, *DOWN, later=down),
    ]
    x_press = send(press.at[pl.ds(NX - 1, 1)], PR.at[pl.ds(0, 1), rows], X, 4, *UP, later=up)
    start(up, down, True)
    x_cells = [
        send(flags.at[last4], FL.at[xlow, rows], X, 0, *direct_up, later=up),
        send(visc.at[last4], VI.at[xlow, rows], X, 2, *direct_up, later=up),
        send(flags.at[first3], FL.at[xhigh, rows], X, 1, *direct_down, later=down),
        send(visc.at[first3], VI.at[xhigh, rows], X, 3, *direct_down, later=down),
    ]
    near_up, near_down = up, down
    up, down = [], []
    y_cells = [
        send(flags.at[:, yfirst], FL.at[xown, yhigh], Y, 2, *SOUTH),
        send(visc.at[:, ylast], VI.at[xown, ylow], Y, 3, *NORTH),
        send(visc.at[:, yfirst], VI.at[xown, yhigh], Y, 4, *SOUTH),
    ]
    y_started = [
        send(S.at[w, xown, elast], S.at[w, xown, ylow], Y, 5, *NORTH),
        send(S.at[u, upper, elast], S.at[u, upper, ylow], Y, 6, *NORTH),
        send(S.at[w, xown, efirst], S.at[w, xown, yhigh], Y, 7, *SOUTH),
        send(S.at[u, upper, efirst], S.at[u, upper, yhigh], Y, 8, *SOUTH),
    ]

    y_press()
    y_flags()
    for a, b in blocks(X0, X1, 2):
        fluid, opened, p = pressed(a, b, Y0)
        fluid_low, opened_low, p_low = pressed(a, b, Y0 - 1)
        act = jnp.maximum(fluid, fluid_low) * opened * opened_low
        S[1, a:b, Y0:Y1] = act * (VEL[1, a - X0 : b - X0] - (p - p_low))
    x_started += [
        send(S.at[v, top4, rows], S.at[v, xlow, rows], X, 12, *UP, later=up),
        send(S.at[v, low3, rows], S.at[v, xhigh, rows], X, 13, *DOWN, later=down),
    ]
    start(up, down, True)
    y_started += [
        send(S.at[v, xown, elast], S.at[v, xown, ylow], Y, 9, *NORTH),
        send(S.at[v, xown, efirst], S.at[v, xown, yhigh], Y, 10, *SOUTH),
    ]
    for wait, (_, source, target, n) in zip(far_cells, passing[0] + passing[1]):
        wait()
        to, there = ((gx + 2, gy), pass_up) if n % 2 == 0 else ((gx - 2, gy), pass_down)
        send(source, target, X, n, to, there, None, out=19 + n)
    start(near_up + up, near_down + down, False)

    local[3].wait()
    n = 11
    for wait in x_cells:
        wait()
    for ref in (FL, VI):
        for layers in (xlow, xhigh):
            y_cells.append(send(ref.at[layers, elast], ref.at[layers, ylow], Y, n, *NORTH))
            y_cells.append(send(ref.at[layers, efirst], ref.at[layers, yhigh], Y, n + 1, *SOUTH))
            n += 2
    for wait in x_started:
        wait()
    x_press()
    for layer, below, raw in ((X0, 0, RAW), (X1, NX, RAWIN)):
        f, g = FL[layer : layer + 1, Y0:Y1], FL[layer - 1 : layer, Y0:Y1]
        act = jnp.maximum(is_fluid(f), is_fluid(g)) * is_open(f) * is_open(g)
        S[0, layer : layer + 1, Y0:Y1] = act * (raw[...] + PR[below : below + 1, Y0:Y1] * is_fluid(g))
    lowest = pl.ds(X0, 1)
    for there, at in ((S, (slice(None), xlow)), (S, (slice(None), xhigh)), (S, (0, lowest))):
        y_started.append(send(there.at[(*at, elast)], there.at[(*at, ylow)], Y, n, *NORTH))
        y_started.append(send(there.at[(*at, efirst)], there.at[(*at, yhigh)], Y, n + 1, *SOUTH))
        n += 2
    for wait in y_cells:
        wait()

    for a, b in blocks(1, EX, 5):
        f = is_fluid(FL[a - 1 : b])
        m = VI[a - 1 : b]
        fx, mx = jnp.maximum(f[1:], f[:-1]), m[1:] + m[:-1]
        fc, mc = f[1:], m[1:]
        if a == 1:
            CW[0] = 2.0 * m[0] * f[0]
        CW[a:b] = 2.0 * mc * fc
        WXY[a:b] = 0.25 * (mx + low_y(mx)) * jnp.maximum(fx, low_y(fx))
        WXZ[a:b] = 0.25 * (mx + low_z(mx)) * jnp.maximum(fx, low_z(fx))
        fy, my = jnp.maximum(fc, low_y(fc)), mc + low_y(mc)
        WYZ[a:b] = 0.25 * (my + low_z(my)) * jnp.maximum(fy, low_z(fy))
        top = lanes(fx) == NZ - 1
        EU[a:b] = jnp.where(top, 0.25 * mx * fx, 0.0)
        EV[a:b] = jnp.where(top, 0.25 * my * fy, 0.0)
    for a, b in blocks(1, EX - 1, 5):
        f = FL[a - 1 : b]
        fluid, opened = is_fluid(f), is_open(f)
        fc, oc = fluid[1:], opened[1:]
        cw = CW[a:b]
        wxy, wxz, wyz = WXY[a : b + 1], WXZ[a : b + 1], WYZ[a:b]
        xy, xz = wxy[:-1], wxz[:-1]
        act = jnp.maximum(fc, fluid[:-1]) * oc * opened[:-1]
        DU[a:b] = act / (1.0 + cw + CW[a - 1 : b - 1] + xy + next_y(xy) + xz + next_z(xz) + EU[a:b])
        act = jnp.maximum(fc, low_y(fc)) * oc * low_y(oc)
        DV[a:b] = act / (1.0 + cw + low_y(cw) + xy + wxy[1:] + wyz + next_z(wyz) + EV[a:b])
        act = jnp.maximum(fc, low_z(fc)) * oc * low_z(oc)
        DW[a:b] = act / (1.0 + cw + low_z(cw) + xz + wxz[1:] + wyz + next_y(wyz))

    for wait in y_started:
        wait()

    def gradient(F, a, b):
        u, v, w = F[0, a - 1 : b + 1], F[1, a - 1 : b + 1], F[2, a - 1 : b + 1]
        uc, vc, wc = u[1:-1], v[1:-1], w[1:-1]
        sx = CW[a - 1 : b] * (u[1:] - u[:-1])
        un, vn, wn = u[1:], v[1:], w[1:]
        xy = WXY[a : b + 1] * (un - low_y(un) + vn - v[:-1])
        xz = WXZ[a : b + 1] * (un - low_z(un) + wn - w[:-1])
        cw = CW[a:b]
        sy = cw * (next_y(vc) - vc)
        sz = cw * (next_z(wc) - wc)
        yz = WYZ[a:b] * (vc - low_z(vc) + wc - low_y(wc))
        xyc, xzc = xy[:-1], xz[:-1]
        return (
            sx[:-1] - sx[1:] + xyc - next_y(xyc) + xzc - next_z(xzc) + EU[a:b] * uc,
            low_y(sy) - sy + xyc - xy[1:] + yz - next_z(yz) + EV[a:b] * vc,
            low_z(sz) - sz + xzc - xz[1:] + yz - next_y(yz),
        ), (uc, vc, wc)

    D = (DU, DV, DW)
    row = lax.broadcasted_iota(jnp.int32, (1, EY, NZ), 1)
    inside = (row >= Y0) & (row < Y1)

    def partial(values, a, b, mask):
        lo, hi = max(a, X0), min(b, X1)
        if lo >= hi:
            return jnp.zeros((1, EY, NZ), F32)
        part = values[lo - a : hi - a]
        return jnp.where(mask, jnp.sum(part, axis=0, keepdims=True), 0.0)

    zero = jnp.zeros((1, EY, NZ), F32)
    b0 = h00 = h01 = h11 = h12 = h22 = zero
    for a, b in blocks(1, EX - 1, 4):
        grad, _ = gradient(S, a, b)
        total = 0.0
        for c in range(3):
            z = -D[c][a:b] * grad[c]
            V0[c, a:b] = z
            total = total - z * grad[c]
        b0 = b0 + partial(total, a, b, inside)
    for a, b in blocks(2, EX - 2, 4):
        grad, field = gradient(V0, a, b)
        same = cross = 0.0
        for c in range(3):
            g = field[c] + grad[c]
            z = D[c][a:b] * g - field[c]
            V1[c, a:b] = z
            same, cross = same + field[c] * g, cross + z * g
        h00, h01 = h00 + partial(same, a, b, inside), h01 + partial(cross, a, b, inside)
    for a, b in blocks(3, EX - 3, 4):
        grad, field = gradient(V1, a, b)
        same = cross = 0.0
        for c in range(3):
            g = field[c] + grad[c]
            z = D[c][a:b] * g - field[c]
            V2[c, a:b] = z
            same, cross = same + field[c] * g, cross + z * g
        h11, h12 = h11 + partial(same, a, b, inside), h12 + partial(cross, a, b, inside)
    edge = row == Y1
    upto = inside | (edge & jnp.logical_not(has_yhi))
    below = ((row >= Y0 - 1) & (row < Y1 - 1)) | ((row == Y1 - 1) & jnp.logical_not(has_yhi))
    for a, b in blocks(X0, X1 + 1, 5):
        u, v, w = V2[0, a - 1 : b], V2[1, a - 1 : b], V2[2, a - 1 : b]
        uc, vc, wc = u[1:], v[1:], w[1:]
        cw = CW[a - 1 : b]
        dx = uc - u[:-1]
        xy = uc - low_y(uc) + vc - v[:-1]
        xz = uc - low_z(uc) + wc - w[:-1]
        yz = vc - low_z(vc) + wc - low_y(wc)
        dz = next_z(wc) - wc
        dy = next_y(vc) - vc
        most = (
            cw[:-1] * dx * dx + WXY[a:b] * xy * xy + WXZ[a:b] * xz * xz + WYZ[a:b] * yz * yz
            + cw[1:] * dz * dz + (1.0 + EU[a:b]) * uc * uc + (1.0 + EV[a:b]) * vc * vc + wc * wc
        )
        along = cw[1:] * dy * dy
        value = jnp.where(upto, most, 0.0) + jnp.where(below, along, 0.0)
        h22 = h22 + jnp.sum(value[: min(b, X1) - a], axis=0, keepdims=True)
        if b > X1:
            h22 = h22 + jnp.where(has_xhi, 0.0, value[X1 - a : X1 - a + 1])

    lane = lax.broadcasted_iota(jnp.int32, (1, NZ), 1)
    payload = jnp.zeros((1, NZ), F32)
    for k, value in enumerate((b0, h00, h01, h11, h12, h22)):
        total = jnp.sum(jnp.sum(value[0], axis=0, keepdims=True), axis=1, keepdims=True)
        payload = jnp.where(lane == k, total, payload)

    def gather(slots, me, peers, n, value, meanwhile):
        slots[me] = value
        for device in peers:
            pltpu.make_async_remote_copy(
                src_ref=slots.at[me], dst_ref=slots.at[me], send_sem=gs.at[n], recv_sem=gr.at[n],
                device_id=device, device_id_type=MESH,
            ).start()
        rest = slots.at[pl.ds(0, len(peers))]
        every = pltpu.make_async_remote_copy(
            src_ref=rest, dst_ref=rest, send_sem=gs.at[n], recv_sem=gr.at[n],
            device_id=peers[0], device_id_type=MESH,
        )
        meanwhile()
        every.wait_recv()
        total = slots[0]
        for r in range(1, len(peers) + 1):
            total = total + slots[r]
        return total, every.wait_send

    def finish_sent():
        for there, copy in sent:
            pl.when(there)(copy.wait_send)

    total, finish_cards = gather(CARDS, card, card_peers, 0, payload, finish_sent)
    total, finish_rings = gather(RINGS, ring, ring_peers, 1, total, finish_cards)

    wide = jnp.broadcast_to(total, (8, NZ))
    at = lax.broadcasted_iota(jnp.int32, (8, NZ), 1)
    m = [
        jnp.broadcast_to(jnp.sum(jnp.where(at == k, wide, 0.0), axis=1, keepdims=True), (8, NZ))
        for k in range(6)
    ]
    r0, a00, a01, a11, a12, a22 = m
    r1 = a00 - r0
    r2 = a01 - r1
    a02 = a11
    tiny = 1e-6

    def over(top, pivot, size):
        good = pivot > tiny * size
        return jnp.where(good, top / jnp.where(good, pivot, 1.0), 0.0)

    d0 = a00
    l10, l20 = over(a01, d0, 0.0), over(a02, d0, 0.0)
    d1 = a11 - l10 * a01
    e21 = a12 - l20 * a01
    l21 = over(e21, d1, a11)
    d2 = a22 - l20 * a02 - l21 * e21
    y1 = r1 - l10 * r0
    y2 = r2 - l20 * r0 - l21 * y1
    c2 = over(y2, d2, a22)
    c1 = over(y1, d1, a11) - l21 * c2
    c0 = over(r0, d0, 0.0) - l10 * c1 - l20 * c2
    c0, c1, c2 = c0[0:1], c1[0:1], c2[0:1]
    for c in range(3):
        for a, b in blocks(X0, X1, 4):
            out[c, a - X0 : b - X0] = (
                S[c, a:b, Y0:Y1] + c0 * V0[c, a:b, Y0:Y1] + c1 * V1[c, a:b, Y0:Y1] + c2 * V2[c, a:b, Y0:Y1]
            )
    finish_rings()


def solution(mesh):
    gxn, gyn = mesh.shape["gx"], mesh.shape["gy"]
    block, cells = P(None, "gx", "gy", None), P("gx", "gy", None)
    ext = (EX, EY, NZ)
    field = lambda *shape: pltpu.VMEM(shape, F32)
    dma = lambda n: pltpu.SemaphoreType.DMA((n,))

    def local(velocity, viscosity, pressure, flags):
        def body(*refs):
            kernel(gxn, gyn, *refs)

        return pl.pallas_call(
            body,
            out_shape=jax.ShapeDtypeStruct((3, NX, NY, NZ), F32),
            in_specs=[pl.BlockSpec(memory_space=pl.ANY)] * 4,
            out_specs=pl.BlockSpec(memory_space=pltpu.VMEM),
            scratch_shapes=[
                *[field(3, *ext)] * 4, field(3, NX, NY, NZ), field(*ext), pltpu.VMEM(ext, jnp.int32),
                field(NX + 1, EY, NZ), field(1, NY, NZ), field(1, NY, NZ),
                field(LOW, NY, NZ), pltpu.VMEM((LOW, NY, NZ), jnp.int32), field(HIGH, NY, NZ),
                pltpu.VMEM((HIGH, NY, NZ), jnp.int32), field(1, NY, NZ),
                *[field(*ext)] * 9,
                field(CARD, 1, NZ), field(RING, 1, NZ),
                dma(4), dma(24), dma(19), dma(25), dma(25), dma(2), dma(2),
            ],
            compiler_params=pltpu.CompilerParams(
                collective_id=1, has_side_effects=True, vmem_limit_bytes=48 * 2**20
            ),
        )(*[pltpu.with_memory_space_constraint(a, pltpu.HBM) for a in (velocity, viscosity, pressure, flags)])

    return jax.shard_map(local, mesh=mesh, in_specs=(block, cells, cells, cells), out_specs=block, check_vma=False)
```

```python
import jax
import jax.numpy as jnp
from jax import lax
from jax.experimental import pallas as pl
from jax.experimental.pallas import tpu as pltpu
from jax.sharding import PartitionSpec as P

MESH = pl.DeviceIdType.MESH
F32 = jnp.float32
NX, NY, NZ = 8, 16, 128
LOW, HIGH = 4, 3
EX, EY = NX + LOW + HIGH, 24
X0, X1 = LOW, LOW + NX
Y0, Y1 = LOW, LOW + NY
CARD, RING = 32, 16


def low_y(a):
    return pltpu.roll(a, 1, 1)


def next_y(a):
    return pltpu.roll(a, EY - 1, 1)


def lanes(a):
    return lax.broadcasted_iota(jnp.int32, a.shape, a.ndim - 1)


def low_z(a):
    return jnp.where(lanes(a) == 0, 0.0, pltpu.roll(a, 1, a.ndim - 1))


def next_z(a):
    return jnp.where(lanes(a) == NZ - 1, 0.0, pltpu.roll(a, NZ - 1, a.ndim - 1))


def blocks(start, stop, size):
    count = -(-(stop - start) // size)
    edges = [start + (stop - start) * n // count for n in range(count + 1)]
    return list(zip(edges[:-1], edges[1:]))


def kernel(
    gxn, gyn,
    vel, visc, press, flags, out,
    S, V0, V1, V2, VEL, VI, FL, PR, RAW, RAWIN, VIA, FLA, VIB, FLB, PRA,
    CW, WXY, WXZ, WYZ, EU, EV, DU, DV, DW,
    CARDS, RINGS,
    lsem, xs, xr, ys, yr, gs, gr,
):
    gx, gy = lax.axis_index("gx"), lax.axis_index("gy")
    has_xlo, has_xhi = gx > 0, gx < gxn - 1
    has_ylo, has_yhi = gy > 0, gy < gyn - 1
    xlo, xhi = (gx - 1, gy), (gx + 1, gy)
    ylo, yhi = (gx, gy - 1), (gx, gy + 1)
    px, zh, py = gx // 8, lax.rem(gx // 4, 2), lax.rem(gx, 4)
    zl, core = gy // 2, lax.rem(gy, 2)
    card = (px * 4 + py) * 2 + core
    ring = zh * 8 + zl

    def hops(d, n):
        return min(d, n - d)

    steps = [(dx, dy, dc) for dx in range(4) for dy in range(4) for dc in range(2)]
    steps.sort(key=lambda d: -(hops(d[0], 4) + hops(d[1], 4) + 0.3 * d[2]))
    pxs, pys, cores = [lax.rem(px + d, 4) * 8 for d in range(4)], [lax.rem(py + d, 4) for d in range(4)], (core, 1 - core)
    card_peers = [(pxs[dx] + zh * 4 + pys[dy], zl * 2 + cores[dc]) for dx, dy, dc in steps[:-1]]
    ring_peers = []
    for d in sorted(range(1, RING), key=lambda d: -hops(d, RING)):
        z = lax.rem(ring + d, RING)
        ring_peers.append((px * 8 + (z // 8) * 4 + py, lax.rem(z, 8) * 2 + core))

    own = (pl.ds(X0, NX), pl.ds(Y0, NY))
    local = [
        pltpu.make_async_copy(flags, FL.at[own], lsem.at[0]),
        pltpu.make_async_copy(press, PR.at[pl.ds(1, NX), pl.ds(Y0, NY)], lsem.at[1]),
        pltpu.make_async_copy(vel, VEL, lsem.at[2]),
        pltpu.make_async_copy(visc, VI.at[own], lsem.at[3]),
    ]
    for copy in local:
        copy.start()

    @pl.when((gx == 0) | (gx == gxn - 1) | (gy == 0) | (gy == gyn - 1))
    def _():
        for ref in (S.at[0], S.at[1], S.at[2], VI, FL):
            ref[0:X0] = jnp.zeros((X0, EY, NZ), ref.dtype)
            ref[X1:EX] = jnp.zeros((EX - X1, EY, NZ), ref.dtype)
            ref[X0:X1, 0:Y0] = jnp.zeros((NX, Y0, NZ), ref.dtype)
            ref[X0:X1, Y1:EY] = jnp.zeros((NX, EY - Y1, NZ), ref.dtype)
        PR[0] = jnp.zeros((EY, NZ), F32)
        PR[1:, 0:Y0] = jnp.zeros((NX, Y0, NZ), F32)
        RAWIN[...] = jnp.zeros((1, NY, NZ), F32)
        for c in range(3):
            V2[c, X1] = jnp.zeros((EY, NZ), F32)

    barrier = pltpu.get_barrier_semaphore()

    def greet(device):
        pl.semaphore_signal(barrier, inc=1, device_id=device, device_id_type=MESH)

    far_up, far_down = (py == 3) & has_xhi, (py == 0) & has_xlo
    pass_up, pass_down = (py == 2) & (gx < gxn - 2), (py == 1) & (gx >= 2)
    near = [
        (far_up, xhi), (far_down, xlo), (pass_up | far_up, (gx + 2, gy)), (pass_down | far_down, (gx - 2, gy)),
        (has_xlo & (py != 0), xlo), (has_xhi & (py != 3), xhi), (has_ylo, ylo), (has_yhi, yhi),
    ]
    for there, device in near:
        pl.when(there)(lambda device=device: greet(device))

    for device in ring_peers + card_peers:
        greet(device)

    def is_fluid(f):
        return jnp.where(f == 1, 1.0, 0.0)

    def is_open(f):
        return jnp.where(f != 0, 1.0, 0.0)

    def pressed(a, b, y):
        f = FL[a:b, y : y + NY]
        fluid = is_fluid(f)
        return fluid, is_open(f), PR[a - LOW + 1 : b - LOW + 1, y : y + NY] * fluid

    for copy in local[:3]:
        copy.wait()
    for a, b in blocks(X0, X1, 2):
        fluid, opened, p = pressed(a, b, Y0)
        act = jnp.maximum(fluid, low_z(fluid)) * opened * low_z(opened)
        S[2, a:b, Y0:Y1] = act * (VEL[2, a - X0 : b - X0] - (p - low_z(p)))
        if a == X0:
            RAW[...] = VEL[0, 0:1] - p[0:1]
            fluid, opened, p, a = fluid[1:], opened[1:], p[1:], a + 1
        fluid_low, opened_low, p_low = pressed(a - 1, b - 1, Y0)
        act = jnp.maximum(fluid, fluid_low) * opened * opened_low
        S[0, a:b, Y0:Y1] = act * (VEL[0, a - X0 : b - X0] - (p - p_low))

    one = lambda there: jnp.where(there, 1, 0)
    pl.semaphore_wait(barrier, CARD + RING - 2 + sum(one(t) for t, _ in near))

    sent = []

    def send(source, target, sems, n, to, there, from_, out=None, later=None):
        copy = pltpu.make_async_remote_copy(
            src_ref=source, dst_ref=target, send_sem=sems[0].at[n if out is None else out], recv_sem=sems[1].at[n],
            device_id=to, device_id_type=MESH,
        )
        if later is None:
            pl.when(there)(copy.start)
        else:
            later.append((there, copy))
        sent.append((there, copy))
        return lambda: pl.when(from_)(copy.wait_recv)

    X, Y = (xs, xr), (ys, yr)
    UP, DOWN = (xhi, has_xhi, has_xlo), (xlo, has_xlo, has_xhi)
    NORTH, SOUTH = (yhi, has_yhi, has_ylo), (ylo, has_ylo, has_yhi)
    rows = pl.ds(Y0, NY)
    last4, first3 = pl.ds(NX - LOW, LOW), pl.ds(0, HIGH)
    xlow, xhigh, xown = pl.ds(0, LOW), pl.ds(X1, HIGH), pl.ds(X0, NX)
    ylow, yhigh = pl.ds(0, LOW), pl.ds(Y1, HIGH)
    ylast, yfirst = pl.ds(NY - LOW, LOW), pl.ds(0, HIGH)
    elast, efirst = pl.ds(Y1 - LOW, LOW), pl.ds(Y0, HIGH)

    def start(up, down, far):
        for copies, crosses in ((up, py == 3), (down, py == 0)):
            for there, copy in copies:
                pl.when(there & (crosses if far else jnp.logical_not(crosses)))(copy.start)

    up, down = [], []
    y_press = send(press.at[:, pl.ds(NY - 1, 1)], PR.at[pl.ds(1, NX), pl.ds(Y0 - 1, 1)], Y, 0, *NORTH)
    y_flags = send(flags.at[:, ylast], FL.at[xown, ylow], Y, 1, *NORTH)
    u, v, w = 0, 1, 2
    upper = pl.ds(X0 + 1, NX - 1)
    top4, low3 = pl.ds(X1 - LOW, LOW), pl.ds(X0, HIGH)
    passing = [
        (flags.at[last4], FLA, FL.at[xlow, rows], 0),
        (visc.at[last4], VIA, VI.at[xlow, rows], 2),
    ], [
        (flags.at[first3], FLB, FL.at[xhigh, rows], 1),
        (visc.at[first3], VIB, VI.at[xhigh, rows], 3),
    ]
    far_cells = [send(part[0], part[1], X, (9, 10, 14)[k], xlo, far_up, pass_up) for k, part in enumerate(passing[0])]
    far_cells += [send(part[0], part[1], X, 17 + k, xhi, far_down, pass_down) for k, part in enumerate(passing[1])]
    direct_up, direct_down = (xhi, has_xhi & (py != 3), has_xlo), (xlo, has_xlo & (py != 0), has_xhi)
    x_started = [
        send(S.at[u, top4, rows], S.at[u, xlow, rows], X, 5, *UP, later=up),
        send(S.at[w, top4, rows], S.at[w, xlow, rows], X, 6, *UP, later=up),
        send(RAW, RAWIN, X, 8, *DOWN, later=down),
        send(S.at[u, pl.ds(X0 + 1, HIGH - 1), rows], S.at[u, pl.ds(X1 + 1, HIGH - 1), rows], X, 7, *DOWN, later=down),
        send(S.at[w, low3, rows], S.at[w, xhigh, rows], X, 11, *DOWN, later=down),
    ]
    x_press = send(press.at[pl.ds(NX - 1, 1)], PR.at[pl.ds(0, 1), rows], X, 4, *UP, later=up)
    start(up, down, True)
    x_cells = [
        send(flags.at[last4], FL.at[xlow, rows], X, 0, *direct_up, later=up),
        send(visc.at[last4], VI.at[xlow, rows], X, 2, *direct_up, later=up),
        send(flags.at[first3], FL.at[xhigh, rows], X, 1, *direct_down, later=down),
        send(visc.at[first3], VI.at[xhigh, rows], X, 3, *direct_down, later=down),
    ]
    near_up, near_down = up, down
    up, down = [], []
    y_press()
    y_flags()
    for a, b in blocks(X0, X1, 2):
        fluid, opened, p = pressed(a, b, Y0)
        fluid_low, opened_low, p_low = pressed(a, b, Y0 - 1)
        act = jnp.maximum(fluid, fluid_low) * opened * opened_low
        S[1, a:b, Y0:Y1] = act * (VEL[1, a - X0 : b - X0] - (p - p_low))
    x_started += [
        send(S.at[v, top4, rows], S.at[v, xlow, rows], X, 12, *UP, later=up),
        send(S.at[v, low3, rows], S.at[v, xhigh, rows], X, 13, *DOWN, later=down),
    ]
    start(up, down, True)
    for wait, (_, source, target, n) in zip(far_cells, passing[0] + passing[1]):
        wait()
        to, there = ((gx + 2, gy), pass_up) if n % 2 == 0 else ((gx - 2, gy), pass_down)
        send(source, target, X, n, to, there, None, out=19 + n)
    start(near_up + up, near_down + down, False)
    y_cells = [
        send(flags.at[:, yfirst], FL.at[xown, yhigh], Y, 2, *SOUTH),
        send(visc.at[:, ylast], VI.at[xown, ylow], Y, 3, *NORTH),
        send(visc.at[:, yfirst], VI.at[xown, yhigh], Y, 4, *SOUTH),
    ]
    y_started = [
        send(S.at[w, xown, elast], S.at[w, xown, ylow], Y, 5, *NORTH),
        send(S.at[u, upper, elast], S.at[u, upper, ylow], Y, 6, *NORTH),
        send(S.at[w, xown, efirst], S.at[w, xown, yhigh], Y, 7, *SOUTH),
        send(S.at[u, upper, efirst], S.at[u, upper, yhigh], Y, 8, *SOUTH),
    ]
    y_started += [
        send(S.at[v, xown, elast], S.at[v, xown, ylow], Y, 9, *NORTH),
        send(S.at[v, xown, efirst], S.at[v, xown, yhigh], Y, 10, *SOUTH),
    ]

    local[3].wait()
    n = 11
    for wait in x_cells:
        wait()
    for ref in (FL, VI):
        for layers in (xlow, xhigh):
            y_cells.append(send(ref.at[layers, elast], ref.at[layers, ylow], Y, n, *NORTH))
            y_cells.append(send(ref.at[layers, efirst], ref.at[layers, yhigh], Y, n + 1, *SOUTH))
            n += 2
    for wait in x_started:
        wait()
    x_press()
    for layer, below, raw in ((X0, 0, RAW), (X1, NX, RAWIN)):
        f, g = FL[layer : layer + 1, Y0:Y1], FL[layer - 1 : layer, Y0:Y1]
        act = jnp.maximum(is_fluid(f), is_fluid(g)) * is_open(f) * is_open(g)
        S[0, layer : layer + 1, Y0:Y1] = act * (raw[...] + PR[below : below + 1, Y0:Y1] * is_fluid(g))
    lowest = pl.ds(X0, 1)
    for there, at in ((S, (slice(None), xlow)), (S, (slice(None), xhigh)), (S, (0, lowest))):
        y_started.append(send(there.at[(*at, elast)], there.at[(*at, ylow)], Y, n, *NORTH))
        y_started.append(send(there.at[(*at, efirst)], there.at[(*at, yhigh)], Y, n + 1, *SOUTH))
        n += 2
    for wait in y_cells:
        wait()

    for a, b in blocks(1, EX, 5):
        f = is_fluid(FL[a - 1 : b])
        m = VI[a - 1 : b]
        fx, mx = jnp.maximum(f[1:], f[:-1]), m[1:] + m[:-1]
        fc, mc = f[1:], m[1:]
        if a == 1:
            CW[0] = 2.0 * m[0] * f[0]
        CW[a:b] = 2.0 * mc * fc
        WXY[a:b] = 0.25 * (mx + low_y(mx)) * jnp.maximum(fx, low_y(fx))
        WXZ[a:b] = 0.25 * (mx + low_z(mx)) * jnp.maximum(fx, low_z(fx))
        fy, my = jnp.maximum(fc, low_y(fc)), mc + low_y(mc)
        WYZ[a:b] = 0.25 * (my + low_z(my)) * jnp.maximum(fy, low_z(fy))
        top = lanes(fx) == NZ - 1
        EU[a:b] = jnp.where(top, 0.25 * mx * fx, 0.0)
        EV[a:b] = jnp.where(top, 0.25 * my * fy, 0.0)
    for a, b in blocks(1, EX - 1, 5):
        f = FL[a - 1 : b]
        fluid, opened = is_fluid(f), is_open(f)
        fc, oc = fluid[1:], opened[1:]
        cw = CW[a:b]
        wxy, wxz, wyz = WXY[a : b + 1], WXZ[a : b + 1], WYZ[a:b]
        xy, xz = wxy[:-1], wxz[:-1]
        act = jnp.maximum(fc, fluid[:-1]) * oc * opened[:-1]
        DU[a:b] = act / (1.0 + cw + CW[a - 1 : b - 1] + xy + next_y(xy) + xz + next_z(xz) + EU[a:b])
        act = jnp.maximum(fc, low_y(fc)) * oc * low_y(oc)
        DV[a:b] = act / (1.0 + cw + low_y(cw) + xy + wxy[1:] + wyz + next_z(wyz) + EV[a:b])
        act = jnp.maximum(fc, low_z(fc)) * oc * low_z(oc)
        DW[a:b] = act / (1.0 + cw + low_z(cw) + xz + wxz[1:] + wyz + next_y(wyz))

    for wait in y_started:
        wait()

    def gradient(F, a, b):
        u, v, w = F[0, a - 1 : b + 1], F[1, a - 1 : b + 1], F[2, a - 1 : b + 1]
        uc, vc, wc = u[1:-1], v[1:-1], w[1:-1]
        sx = CW[a - 1 : b] * (u[1:] - u[:-1])
        un, vn, wn = u[1:], v[1:], w[1:]
        xy = WXY[a : b + 1] * (un - low_y(un) + vn - v[:-1])
        xz = WXZ[a : b + 1] * (un - low_z(un) + wn - w[:-1])
        cw = CW[a:b]
        sy = cw * (next_y(vc) - vc)
        sz = cw * (next_z(wc) - wc)
        yz = WYZ[a:b] * (vc - low_z(vc) + wc - low_y(wc))
        xyc, xzc = xy[:-1], xz[:-1]
        return (
            sx[:-1] - sx[1:] + xyc - next_y(xyc) + xzc - next_z(xzc) + EU[a:b] * uc,
            low_y(sy) - sy + xyc - xy[1:] + yz - next_z(yz) + EV[a:b] * vc,
            low_z(sz) - sz + xzc - xz[1:] + yz - next_y(yz),
        ), (uc, vc, wc)

    D = (DU, DV, DW)
    row = lax.broadcasted_iota(jnp.int32, (1, EY, NZ), 1)
    inside = (row >= Y0) & (row < Y1)

    def partial(values, a, b, mask):
        lo, hi = max(a, X0), min(b, X1)
        if lo >= hi:
            return jnp.zeros((1, EY, NZ), F32)
        part = values[lo - a : hi - a]
        return jnp.where(mask, jnp.sum(part, axis=0, keepdims=True), 0.0)

    zero = jnp.zeros((1, EY, NZ), F32)
    b0 = h00 = h01 = h11 = h12 = h22 = zero
    for a, b in blocks(1, EX - 1, 7):
        grad, _ = gradient(S, a, b)
        total = 0.0
        for c in range(3):
            z = -D[c][a:b] * grad[c]
            V0[c, a:b] = z
            total = total - z * grad[c]
        b0 = b0 + partial(total, a, b, inside)
    for a, b in blocks(2, EX - 2, 6):
        grad, field = gradient(V0, a, b)
        same = cross = 0.0
        for c in range(3):
            g = field[c] + grad[c]
            z = D[c][a:b] * g - field[c]
            V1[c, a:b] = z
            same, cross = same + field[c] * g, cross + z * g
        h00, h01 = h00 + partial(same, a, b, inside), h01 + partial(cross, a, b, inside)
    for a, b in blocks(3, EX - 3, 5):
        grad, field = gradient(V1, a, b)
        same = cross = 0.0
        for c in range(3):
            g = field[c] + grad[c]
            z = D[c][a:b] * g - field[c]
            V2[c, a:b] = z
            same, cross = same + field[c] * g, cross + z * g
        h11, h12 = h11 + partial(same, a, b, inside), h12 + partial(cross, a, b, inside)
    edge = row == Y1
    upto = inside | (edge & jnp.logical_not(has_yhi))
    below = ((row >= Y0 - 1) & (row < Y1 - 1)) | ((row == Y1 - 1) & jnp.logical_not(has_yhi))
    for a, b in blocks(X0, X1 + 1, 5):
        u, v, w = V2[0, a - 1 : b], V2[1, a - 1 : b], V2[2, a - 1 : b]
        uc, vc, wc = u[1:], v[1:], w[1:]
        cw = CW[a - 1 : b]
        dx = uc - u[:-1]
        xy = uc - low_y(uc) + vc - v[:-1]
        xz = uc - low_z(uc) + wc - w[:-1]
        yz = vc - low_z(vc) + wc - low_y(wc)
        dz = next_z(wc) - wc
        dy = next_y(vc) - vc
        most = (
            cw[:-1] * dx * dx + WXY[a:b] * xy * xy + WXZ[a:b] * xz * xz + WYZ[a:b] * yz * yz
            + cw[1:] * dz * dz + (1.0 + EU[a:b]) * uc * uc + (1.0 + EV[a:b]) * vc * vc + wc * wc
        )
        along = cw[1:] * dy * dy
        value = jnp.where(upto, most, 0.0) + jnp.where(below, along, 0.0)
        h22 = h22 + jnp.sum(value[: min(b, X1) - a], axis=0, keepdims=True)
        if b > X1:
            h22 = h22 + jnp.where(has_xhi, 0.0, value[X1 - a : X1 - a + 1])

    lane = lax.broadcasted_iota(jnp.int32, (1, NZ), 1)
    payload = jnp.zeros((1, NZ), F32)
    for k, value in enumerate((b0, h00, h01, h11, h12, h22)):
        total = jnp.sum(jnp.sum(value[0], axis=0, keepdims=True), axis=1, keepdims=True)
        payload = jnp.where(lane == k, total, payload)

    def gather(slots, me, peers, n, value, meanwhile):
        slots[me] = value
        for device in peers:
            pltpu.make_async_remote_copy(
                src_ref=slots.at[me], dst_ref=slots.at[me], send_sem=gs.at[n], recv_sem=gr.at[n],
                device_id=device, device_id_type=MESH,
            ).start()
        rest = slots.at[pl.ds(0, len(peers))]
        every = pltpu.make_async_remote_copy(
            src_ref=rest, dst_ref=rest, send_sem=gs.at[n], recv_sem=gr.at[n],
            device_id=peers[0], device_id_type=MESH,
        )
        meanwhile()
        every.wait_recv()
        total = slots[0]
        for r in range(1, len(peers) + 1):
            total = total + slots[r]
        return total, every.wait_send

    def finish_sent():
        for there, copy in sent:
            pl.when(there)(copy.wait_send)

    total, finish_cards = gather(CARDS, card, card_peers, 0, payload, finish_sent)
    total, finish_rings = gather(RINGS, ring, ring_peers, 1, total, finish_cards)

    wide = jnp.broadcast_to(total, (8, NZ))
    at = lax.broadcasted_iota(jnp.int32, (8, NZ), 1)
    m = [
        jnp.broadcast_to(jnp.sum(jnp.where(at == k, wide, 0.0), axis=1, keepdims=True), (8, NZ))
        for k in range(6)
    ]
    r0, a00, a01, a11, a12, a22 = m
    r1 = a00 - r0
    r2 = a01 - r1
    a02 = a11
    tiny = 1e-6

    def over(top, pivot, size):
        good = pivot > tiny * size
        return jnp.where(good, top / jnp.where(good, pivot, 1.0), 0.0)

    d0 = a00
    l10, l20 = over(a01, d0, 0.0), over(a02, d0, 0.0)
    d1 = a11 - l10 * a01
    e21 = a12 - l20 * a01
    l21 = over(e21, d1, a11)
    d2 = a22 - l20 * a02 - l21 * e21
    y1 = r1 - l10 * r0
    y2 = r2 - l20 * r0 - l21 * y1
    c2 = over(y2, d2, a22)
    c1 = over(y1, d1, a11) - l21 * c2
    c0 = over(r0, d0, 0.0) - l10 * c1 - l20 * c2
    c0, c1, c2 = c0[0:1], c1[0:1], c2[0:1]
    for c in range(3):
        for a, b in blocks(X0, X1, 4):
            out[c, a - X0 : b - X0] = (
                S[c, a:b, Y0:Y1] + c0 * V0[c, a:b, Y0:Y1] + c1 * V1[c, a:b, Y0:Y1] + c2 * V2[c, a:b, Y0:Y1]
            )
    finish_rings()


def solution(mesh):
    gxn, gyn = mesh.shape["gx"], mesh.shape["gy"]
    block, cells = P(None, "gx", "gy", None), P("gx", "gy", None)
    ext = (EX, EY, NZ)
    field = lambda *shape: pltpu.VMEM(shape, F32)
    dma = lambda n: pltpu.SemaphoreType.DMA((n,))

    def local(velocity, viscosity, pressure, flags):
        def body(*refs):
            kernel(gxn, gyn, *refs)

        return pl.pallas_call(
            body,
            out_shape=jax.ShapeDtypeStruct((3, NX, NY, NZ), F32),
            in_specs=[pl.BlockSpec(memory_space=pl.ANY)] * 4,
            out_specs=pl.BlockSpec(memory_space=pltpu.VMEM),
            scratch_shapes=[
                *[field(3, *ext)] * 4, field(3, NX, NY, NZ), field(*ext), pltpu.VMEM(ext, jnp.int32),
                field(NX + 1, EY, NZ), field(1, NY, NZ), field(1, NY, NZ),
                field(LOW, NY, NZ), pltpu.VMEM((LOW, NY, NZ), jnp.int32), field(HIGH, NY, NZ),
                pltpu.VMEM((HIGH, NY, NZ), jnp.int32), field(1, NY, NZ),
                *[field(*ext)] * 9,
                field(CARD, 1, NZ), field(RING, 1, NZ),
                dma(4), dma(24), dma(19), dma(25), dma(25), dma(2), dma(2),
            ],
            compiler_params=pltpu.CompilerParams(
                collective_id=1, has_side_effects=True, vmem_limit_bytes=48 * 2**20
            ),
        )(*[pltpu.with_memory_space_constraint(a, pltpu.HBM) for a in (velocity, viscosity, pressure, flags)])

    return jax.shard_map(local, mesh=mesh, in_specs=(block, cells, cells, cells), out_specs=block, check_vma=False)
```

```python
import jax
import jax.numpy as jnp
from jax import lax
from jax.experimental import pallas as pl
from jax.experimental.pallas import tpu as pltpu
from jax.sharding import PartitionSpec as P

MESH = pl.DeviceIdType.MESH
F32 = jnp.float32
NX, NY, NZ = 8, 16, 128
LOW, HIGH = 4, 3
EX, EY = NX + LOW + HIGH, 24
X0, X1 = LOW, LOW + NX
Y0, Y1 = LOW, LOW + NY
CARD, RING = 16, 32


def low_y(a):
    return pltpu.roll(a, 1, 1)


def next_y(a):
    return pltpu.roll(a, EY - 1, 1)


def lanes(a):
    return lax.broadcasted_iota(jnp.int32, a.shape, a.ndim - 1)


def low_z(a):
    return jnp.where(lanes(a) == 0, 0.0, pltpu.roll(a, 1, a.ndim - 1))


def next_z(a):
    return jnp.where(lanes(a) == NZ - 1, 0.0, pltpu.roll(a, NZ - 1, a.ndim - 1))


def blocks(start, stop, size):
    count = -(-(stop - start) // size)
    edges = [start + (stop - start) * n // count for n in range(count + 1)]
    return list(zip(edges[:-1], edges[1:]))


def kernel(
    gxn, gyn,
    vel, visc, press, flags, out,
    S, V0, V1, V2, VEL, VI, FL, PR, RAW, RAWIN, VIA, FLA, VIB, FLB, PRA,
    CW, WXY, WXZ, WYZ, EU, EV, DU, DV, DW,
    CARDS, RINGS,
    lsem, xs, xr, ys, yr, gs, gr,
):
    gx, gy = lax.axis_index("gx"), lax.axis_index("gy")
    has_xlo, has_xhi = gx > 0, gx < gxn - 1
    has_ylo, has_yhi = gy > 0, gy < gyn - 1
    xlo, xhi = (gx - 1, gy), (gx + 1, gy)
    ylo, yhi = (gx, gy - 1), (gx, gy + 1)
    px, zh, py = gx // 8, lax.rem(gx // 4, 2), lax.rem(gx, 4)
    zl, core = gy // 2, lax.rem(gy, 2)
    card = px * 4 + py
    ring = (zh * 8 + zl) * 2 + core

    def hops(d, n):
        return min(d, n - d)

    steps = [(dx, dy, dc) for dx in range(4) for dy in range(4) for dc in range(1)]
    steps.sort(key=lambda d: -(hops(d[0], 4) + hops(d[1], 4) + 0.3 * d[2]))
    pxs, pys, cores = [lax.rem(px + d, 4) * 8 for d in range(4)], [lax.rem(py + d, 4) for d in range(4)], (core, 1 - core)
    card_peers = [(pxs[dx] + zh * 4 + pys[dy], zl * 2 + cores[dc]) for dx, dy, dc in steps[:-1]]
    ring_peers = []
    for d in sorted(range(16), key=lambda d: -hops(d, 16)):
        z = lax.rem(zh * 8 + zl + d, 16)
        ring_peers += [(px * 8 + (z // 8) * 4 + py, lax.rem(z, 8) * 2 + c) for c in (cores if d else cores[1:])]

    own = (pl.ds(X0, NX), pl.ds(Y0, NY))
    local = [
        pltpu.make_async_copy(flags, FL.at[own], lsem.at[0]),
        pltpu.make_async_copy(press, PR.at[pl.ds(1, NX), pl.ds(Y0, NY)], lsem.at[1]),
        pltpu.make_async_copy(vel, VEL, lsem.at[2]),
        pltpu.make_async_copy(visc, VI.at[own], lsem.at[3]),
    ]
    for copy in local:
        copy.start()

    @pl.when((gx == 0) | (gx == gxn - 1) | (gy == 0) | (gy == gyn - 1))
    def _():
        for ref in (S.at[0], S.at[1], S.at[2], VI, FL):
            ref[0:X0] = jnp.zeros((X0, EY, NZ), ref.dtype)
            ref[X1:EX] = jnp.zeros((EX - X1, EY, NZ), ref.dtype)
            ref[X0:X1, 0:Y0] = jnp.zeros((NX, Y0, NZ), ref.dtype)
            ref[X0:X1, Y1:EY] = jnp.zeros((NX, EY - Y1, NZ), ref.dtype)
        PR[0] = jnp.zeros((EY, NZ), F32)
        PR[1:, 0:Y0] = jnp.zeros((NX, Y0, NZ), F32)
        RAWIN[...] = jnp.zeros((1, NY, NZ), F32)
        for c in range(3):
            V2[c, X1] = jnp.zeros((EY, NZ), F32)

    barrier = pltpu.get_barrier_semaphore()

    def greet(device):
        pl.semaphore_signal(barrier, inc=1, device_id=device, device_id_type=MESH)

    far_up, far_down = (py == 3) & has_xhi, (py == 0) & has_xlo
    pass_up, pass_down = (py == 2) & (gx < gxn - 2), (py == 1) & (gx >= 2)
    near = [
        (far_up, xhi), (far_down, xlo), (pass_up | far_up, (gx + 2, gy)), (pass_down | far_down, (gx - 2, gy)),
        (has_xlo & (py != 0), xlo), (has_xhi & (py != 3), xhi), (has_ylo, ylo), (has_yhi, yhi),
    ]
    for there, device in near:
        pl.when(there)(lambda device=device: greet(device))

    for device in ring_peers + card_peers:
        greet(device)

    def is_fluid(f):
        return jnp.where(f == 1, 1.0, 0.0)

    def is_open(f):
        return jnp.where(f != 0, 1.0, 0.0)

    def pressed(a, b, y):
        f = FL[a:b, y : y + NY]
        fluid = is_fluid(f)
        return fluid, is_open(f), PR[a - LOW + 1 : b - LOW + 1, y : y + NY] * fluid

    for copy in local[:3]:
        copy.wait()
    for a, b in blocks(X0, X1, 2):
        fluid, opened, p = pressed(a, b, Y0)
        act = jnp.maximum(fluid, low_z(fluid)) * opened * low_z(opened)
        S[2, a:b, Y0:Y1] = act * (VEL[2, a - X0 : b - X0] - (p - low_z(p)))
        if a == X0:
            RAW[...] = VEL[0, 0:1] - p[0:1]
            fluid, opened, p, a = fluid[1:], opened[1:], p[1:], a + 1
        fluid_low, opened_low, p_low = pressed(a - 1, b - 1, Y0)
        act = jnp.maximum(fluid, fluid_low) * opened * opened_low
        S[0, a:b, Y0:Y1] = act * (VEL[0, a - X0 : b - X0] - (p - p_low))

    one = lambda there: jnp.where(there, 1, 0)
    pl.semaphore_wait(barrier, CARD + RING - 2 + sum(one(t) for t, _ in near))

    sent = []

    def send(source, target, sems, n, to, there, from_, out=None, later=None):
        copy = pltpu.make_async_remote_copy(
            src_ref=source, dst_ref=target, send_sem=sems[0].at[n if out is None else out], recv_sem=sems[1].at[n],
            device_id=to, device_id_type=MESH,
        )
        if later is None:
            pl.when(there)(copy.start)
        else:
            later.append((there, copy))
        sent.append((there, copy))
        return lambda: pl.when(from_)(copy.wait_recv)

    X, Y = (xs, xr), (ys, yr)
    UP, DOWN = (xhi, has_xhi, has_xlo), (xlo, has_xlo, has_xhi)
    NORTH, SOUTH = (yhi, has_yhi, has_ylo), (ylo, has_ylo, has_yhi)
    rows = pl.ds(Y0, NY)
    last4, first3 = pl.ds(NX - LOW, LOW), pl.ds(0, HIGH)
    xlow, xhigh, xown = pl.ds(0, LOW), pl.ds(X1, HIGH), pl.ds(X0, NX)
    ylow, yhigh = pl.ds(0, LOW), pl.ds(Y1, HIGH)
    ylast, yfirst = pl.ds(NY - LOW, LOW), pl.ds(0, HIGH)
    elast, efirst = pl.ds(Y1 - LOW, LOW), pl.ds(Y0, HIGH)

    def start(up, down, far):
        for copies, crosses in ((up, py == 3), (down, py == 0)):
            for there, copy in copies:
                pl.when(there & (crosses if far else jnp.logical_not(crosses)))(copy.start)

    up, down = [], []
    y_press = send(press.at[:, pl.ds(NY - 1, 1)], PR.at[pl.ds(1, NX), pl.ds(Y0 - 1, 1)], Y, 0, *NORTH)
    y_flags = send(flags.at[:, ylast], FL.at[xown, ylow], Y, 1, *NORTH)
    u, v, w = 0, 1, 2
    upper = pl.ds(X0 + 1, NX - 1)
    top4, low3 = pl.ds(X1 - LOW, LOW), pl.ds(X0, HIGH)
    passing = [
        (flags.at[last4], FLA, FL.at[xlow, rows], 0),
        (visc.at[last4], VIA, VI.at[xlow, rows], 2),
    ], [
        (flags.at[first3], FLB, FL.at[xhigh, rows], 1),
        (visc.at[first3], VIB, VI.at[xhigh, rows], 3),
    ]
    far_cells = [send(part[0], part[1], X, (9, 10, 14)[k], xlo, far_up, pass_up) for k, part in enumerate(passing[0])]
    far_cells += [send(part[0], part[1], X, 17 + k, xhi, far_down, pass_down) for k, part in enumerate(passing[1])]
    direct_up, direct_down = (xhi, has_xhi & (py != 3), has_xlo), (xlo, has_xlo & (py != 0), has_xhi)
    x_started = [
        send(S.at[u, top4, rows], S.at[u, xlow, rows], X, 5, *UP, later=up),
        send(S.at[w, top4, rows], S.at[w, xlow, rows], X, 6, *UP, later=up),
        send(RAW, RAWIN, X, 8, *DOWN, later=down),
        send(S.at[u, pl.ds(X0 + 1, HIGH - 1), rows], S.at[u, pl.ds(X1 + 1, HIGH - 1), rows], X, 7, *DOWN, later=down),
        send(S.at[w, low3, rows], S.at[w, xhigh, rows], X, 11, *DOWN, later=down),
    ]
    x_press = send(press.at[pl.ds(NX - 1, 1)], PR.at[pl.ds(0, 1), rows], X, 4, *UP, later=up)
    start(up, down, True)
    x_cells = [
        send(flags.at[last4], FL.at[xlow, rows], X, 0, *direct_up, later=up),
        send(visc.at[last4], VI.at[xlow, rows], X, 2, *direct_up, later=up),
        send(flags.at[first3], FL.at[xhigh, rows], X, 1, *direct_down, later=down),
        send(visc.at[first3], VI.at[xhigh, rows], X, 3, *direct_down, later=down),
    ]
    near_up, near_down = up, down
    up, down = [], []
    y_press()
    y_flags()
    for a, b in blocks(X0, X1, 2):
        fluid, opened, p = pressed(a, b, Y0)
        fluid_low, opened_low, p_low = pressed(a, b, Y0 - 1)
        act = jnp.maximum(fluid, fluid_low) * opened * opened_low
        S[1, a:b, Y0:Y1] = act * (VEL[1, a - X0 : b - X0] - (p - p_low))
    x_started += [
        send(S.at[v, top4, rows], S.at[v, xlow, rows], X, 12, *UP, later=up),
        send(S.at[v, low3, rows], S.at[v, xhigh, rows], X, 13, *DOWN, later=down),
    ]
    start(up, down, True)
    for wait, (_, source, target, n) in zip(far_cells, passing[0] + passing[1]):
        wait()
        to, there = ((gx + 2, gy), pass_up) if n % 2 == 0 else ((gx - 2, gy), pass_down)
        send(source, target, X, n, to, there, None, out=19 + n)
    start(near_up + up, near_down + down, False)
    y_cells = [
        send(flags.at[:, yfirst], FL.at[xown, yhigh], Y, 2, *SOUTH),
        send(visc.at[:, ylast], VI.at[xown, ylow], Y, 3, *NORTH),
        send(visc.at[:, yfirst], VI.at[xown, yhigh], Y, 4, *SOUTH),
    ]
    y_started = [
        send(S.at[w, xown, elast], S.at[w, xown, ylow], Y, 5, *NORTH),
        send(S.at[u, upper, elast], S.at[u, upper, ylow], Y, 6, *NORTH),
        send(S.at[w, xown, efirst], S.at[w, xown, yhigh], Y, 7, *SOUTH),
        send(S.at[u, upper, efirst], S.at[u, upper, yhigh], Y, 8, *SOUTH),
    ]
    y_started += [
        send(S.at[v, xown, elast], S.at[v, xown, ylow], Y, 9, *NORTH),
        send(S.at[v, xown, efirst], S.at[v, xown, yhigh], Y, 10, *SOUTH),
    ]

    local[3].wait()
    n = 11
    for wait in x_cells:
        wait()
    for ref in (FL, VI):
        for layers in (xlow, xhigh):
            y_cells.append(send(ref.at[layers, elast], ref.at[layers, ylow], Y, n, *NORTH))
            y_cells.append(send(ref.at[layers, efirst], ref.at[layers, yhigh], Y, n + 1, *SOUTH))
            n += 2
    for wait in x_started:
        wait()
    x_press()
    for layer, below, raw in ((X0, 0, RAW), (X1, NX, RAWIN)):
        f, g = FL[layer : layer + 1, Y0:Y1], FL[layer - 1 : layer, Y0:Y1]
        act = jnp.maximum(is_fluid(f), is_fluid(g)) * is_open(f) * is_open(g)
        S[0, layer : layer + 1, Y0:Y1] = act * (raw[...] + PR[below : below + 1, Y0:Y1] * is_fluid(g))
    lowest = pl.ds(X0, 1)
    for there, at in ((S, (slice(None), xlow)), (S, (slice(None), xhigh)), (S, (0, lowest))):
        y_started.append(send(there.at[(*at, elast)], there.at[(*at, ylow)], Y, n, *NORTH))
        y_started.append(send(there.at[(*at, efirst)], there.at[(*at, yhigh)], Y, n + 1, *SOUTH))
        n += 2
    for wait in y_cells:
        wait()

    for a, b in blocks(1, EX, 5):
        f = is_fluid(FL[a - 1 : b])
        m = VI[a - 1 : b]
        fx, mx = jnp.maximum(f[1:], f[:-1]), m[1:] + m[:-1]
        fc, mc = f[1:], m[1:]
        if a == 1:
            CW[0] = 2.0 * m[0] * f[0]
        CW[a:b] = 2.0 * mc * fc
        WXY[a:b] = 0.25 * (mx + low_y(mx)) * jnp.maximum(fx, low_y(fx))
        WXZ[a:b] = 0.25 * (mx + low_z(mx)) * jnp.maximum(fx, low_z(fx))
        fy, my = jnp.maximum(fc, low_y(fc)), mc + low_y(mc)
        WYZ[a:b] = 0.25 * (my + low_z(my)) * jnp.maximum(fy, low_z(fy))
        top = lanes(fx) == NZ - 1
        EU[a:b] = jnp.where(top, 0.25 * mx * fx, 0.0)
        EV[a:b] = jnp.where(top, 0.25 * my * fy, 0.0)
    for a, b in blocks(1, EX - 1, 5):
        f = FL[a - 1 : b]
        fluid, opened = is_fluid(f), is_open(f)
        fc, oc = fluid[1:], opened[1:]
        cw = CW[a:b]
        wxy, wxz, wyz = WXY[a : b + 1], WXZ[a : b + 1], WYZ[a:b]
        xy, xz = wxy[:-1], wxz[:-1]
        act = jnp.maximum(fc, fluid[:-1]) * oc * opened[:-1]
        DU[a:b] = act / (1.0 + cw + CW[a - 1 : b - 1] + xy + next_y(xy) + xz + next_z(xz) + EU[a:b])
        act = jnp.maximum(fc, low_y(fc)) * oc * low_y(oc)
        DV[a:b] = act / (1.0 + cw + low_y(cw) + xy + wxy[1:] + wyz + next_z(wyz) + EV[a:b])
        act = jnp.maximum(fc, low_z(fc)) * oc * low_z(oc)
        DW[a:b] = act / (1.0 + cw + low_z(cw) + xz + wxz[1:] + wyz + next_y(wyz))

    for wait in y_started:
        wait()

    def gradient(F, a, b):
        u, v, w = F[0, a - 1 : b + 1], F[1, a - 1 : b + 1], F[2, a - 1 : b + 1]
        uc, vc, wc = u[1:-1], v[1:-1], w[1:-1]
        sx = CW[a - 1 : b] * (u[1:] - u[:-1])
        un, vn, wn = u[1:], v[1:], w[1:]
        xy = WXY[a : b + 1] * (un - low_y(un) + vn - v[:-1])
        xz = WXZ[a : b + 1] * (un - low_z(un) + wn - w[:-1])
        cw = CW[a:b]
        sy = cw * (next_y(vc) - vc)
        sz = cw * (next_z(wc) - wc)
        yz = WYZ[a:b] * (vc - low_z(vc) + wc - low_y(wc))
        xyc, xzc = xy[:-1], xz[:-1]
        return (
            sx[:-1] - sx[1:] + xyc - next_y(xyc) + xzc - next_z(xzc) + EU[a:b] * uc,
            low_y(sy) - sy + xyc - xy[1:] + yz - next_z(yz) + EV[a:b] * vc,
            low_z(sz) - sz + xzc - xz[1:] + yz - next_y(yz),
        ), (uc, vc, wc)

    D = (DU, DV, DW)
    row = lax.broadcasted_iota(jnp.int32, (1, EY, NZ), 1)
    inside = (row >= Y0) & (row < Y1)

    def partial(values, a, b, mask):
        lo, hi = max(a, X0), min(b, X1)
        if lo >= hi:
            return jnp.zeros((1, EY, NZ), F32)
        part = values[lo - a : hi - a]
        return jnp.where(mask, jnp.sum(part, axis=0, keepdims=True), 0.0)

    zero = jnp.zeros((1, EY, NZ), F32)
    b0 = h00 = h01 = h11 = h12 = h22 = zero
    for a, b in blocks(1, EX - 1, 7):
        grad, _ = gradient(S, a, b)
        total = 0.0
        for c in range(3):
            z = -D[c][a:b] * grad[c]
            V0[c, a:b] = z
            total = total - z * grad[c]
        b0 = b0 + partial(total, a, b, inside)
    for a, b in blocks(2, EX - 2, 6):
        grad, field = gradient(V0, a, b)
        same = cross = 0.0
        for c in range(3):
            g = field[c] + grad[c]
            z = D[c][a:b] * g - field[c]
            V1[c, a:b] = z
            same, cross = same + field[c] * g, cross + z * g
        h00, h01 = h00 + partial(same, a, b, inside), h01 + partial(cross, a, b, inside)
    for a, b in blocks(3, EX - 3, 5):
        grad, field = gradient(V1, a, b)
        same = cross = 0.0
        for c in range(3):
            g = field[c] + grad[c]
            z = D[c][a:b] * g - field[c]
            V2[c, a:b] = z
            same, cross = same + field[c] * g, cross + z * g
        h11, h12 = h11 + partial(same, a, b, inside), h12 + partial(cross, a, b, inside)
    edge = row == Y1
    upto = inside | (edge & jnp.logical_not(has_yhi))
    below = ((row >= Y0 - 1) & (row < Y1 - 1)) | ((row == Y1 - 1) & jnp.logical_not(has_yhi))
    for a, b in blocks(X0, X1 + 1, 5):
        u, v, w = V2[0, a - 1 : b], V2[1, a - 1 : b], V2[2, a - 1 : b]
        uc, vc, wc = u[1:], v[1:], w[1:]
        cw = CW[a - 1 : b]
        dx = uc - u[:-1]
        xy = uc - low_y(uc) + vc - v[:-1]
        xz = uc - low_z(uc) + wc - w[:-1]
        yz = vc - low_z(vc) + wc - low_y(wc)
        dz = next_z(wc) - wc
        dy = next_y(vc) - vc
        most = (
            cw[:-1] * dx * dx + WXY[a:b] * xy * xy + WXZ[a:b] * xz * xz + WYZ[a:b] * yz * yz
            + cw[1:] * dz * dz + (1.0 + EU[a:b]) * uc * uc + (1.0 + EV[a:b]) * vc * vc + wc * wc
        )
        along = cw[1:] * dy * dy
        value = jnp.where(upto, most, 0.0) + jnp.where(below, along, 0.0)
        h22 = h22 + jnp.sum(value[: min(b, X1) - a], axis=0, keepdims=True)
        if b > X1:
            h22 = h22 + jnp.where(has_xhi, 0.0, value[X1 - a : X1 - a + 1])

    lane = lax.broadcasted_iota(jnp.int32, (1, NZ), 1)
    payload = jnp.zeros((1, NZ), F32)
    for k, value in enumerate((b0, h00, h01, h11, h12, h22)):
        total = jnp.sum(jnp.sum(value[0], axis=0, keepdims=True), axis=1, keepdims=True)
        payload = jnp.where(lane == k, total, payload)

    def gather(slots, me, peers, n, value, meanwhile):
        slots[me] = value
        for device in peers:
            pltpu.make_async_remote_copy(
                src_ref=slots.at[me], dst_ref=slots.at[me], send_sem=gs.at[n], recv_sem=gr.at[n],
                device_id=device, device_id_type=MESH,
            ).start()
        rest = slots.at[pl.ds(0, len(peers))]
        every = pltpu.make_async_remote_copy(
            src_ref=rest, dst_ref=rest, send_sem=gs.at[n], recv_sem=gr.at[n],
            device_id=peers[0], device_id_type=MESH,
        )
        meanwhile()
        every.wait_recv()
        total = slots[0]
        for r in range(1, len(peers) + 1):
            total = total + slots[r]
        return total, every.wait_send

    def finish_sent():
        for there, copy in sent:
            pl.when(there)(copy.wait_send)

    total, finish_cards = gather(CARDS, card, card_peers, 0, payload, finish_sent)
    total, finish_rings = gather(RINGS, ring, ring_peers, 1, total, finish_cards)

    wide = jnp.broadcast_to(total, (8, NZ))
    at = lax.broadcasted_iota(jnp.int32, (8, NZ), 1)
    m = [
        jnp.broadcast_to(jnp.sum(jnp.where(at == k, wide, 0.0), axis=1, keepdims=True), (8, NZ))
        for k in range(6)
    ]
    r0, a00, a01, a11, a12, a22 = m
    r1 = a00 - r0
    r2 = a01 - r1
    a02 = a11
    tiny = 1e-6

    def over(top, pivot, size):
        good = pivot > tiny * size
        return jnp.where(good, top / jnp.where(good, pivot, 1.0), 0.0)

    d0 = a00
    l10, l20 = over(a01, d0, 0.0), over(a02, d0, 0.0)
    d1 = a11 - l10 * a01
    e21 = a12 - l20 * a01
    l21 = over(e21, d1, a11)
    d2 = a22 - l20 * a02 - l21 * e21
    y1 = r1 - l10 * r0
    y2 = r2 - l20 * r0 - l21 * y1
    c2 = over(y2, d2, a22)
    c1 = over(y1, d1, a11) - l21 * c2
    c0 = over(r0, d0, 0.0) - l10 * c1 - l20 * c2
    c0, c1, c2 = c0[0:1], c1[0:1], c2[0:1]
    for c in range(3):
        for a, b in blocks(X0, X1, 4):
            out[c, a - X0 : b - X0] = (
                S[c, a:b, Y0:Y1] + c0 * V0[c, a:b, Y0:Y1] + c1 * V1[c, a:b, Y0:Y1] + c2 * V2[c, a:b, Y0:Y1]
            )
    finish_rings()


def solution(mesh):
    gxn, gyn = mesh.shape["gx"], mesh.shape["gy"]
    block, cells = P(None, "gx", "gy", None), P("gx", "gy", None)
    ext = (EX, EY, NZ)
    field = lambda *shape: pltpu.VMEM(shape, F32)
    dma = lambda n: pltpu.SemaphoreType.DMA((n,))

    def local(velocity, viscosity, pressure, flags):
        def body(*refs):
            kernel(gxn, gyn, *refs)

        return pl.pallas_call(
            body,
            out_shape=jax.ShapeDtypeStruct((3, NX, NY, NZ), F32),
            in_specs=[pl.BlockSpec(memory_space=pl.ANY)] * 4,
            out_specs=pl.BlockSpec(memory_space=pltpu.VMEM),
            scratch_shapes=[
                *[field(3, *ext)] * 4, field(3, NX, NY, NZ), field(*ext), pltpu.VMEM(ext, jnp.int32),
                field(NX + 1, EY, NZ), field(1, NY, NZ), field(1, NY, NZ),
                field(LOW, NY, NZ), pltpu.VMEM((LOW, NY, NZ), jnp.int32), field(HIGH, NY, NZ),
                pltpu.VMEM((HIGH, NY, NZ), jnp.int32), field(1, NY, NZ),
                *[field(*ext)] * 9,
                field(CARD, 1, NZ), field(RING, 1, NZ),
                dma(4), dma(24), dma(19), dma(25), dma(25), dma(2), dma(2),
            ],
            compiler_params=pltpu.CompilerParams(
                collective_id=1, has_side_effects=True, vmem_limit_bytes=48 * 2**20
            ),
        )(*[pltpu.with_memory_space_constraint(a, pltpu.HBM) for a in (velocity, viscosity, pressure, flags)])

    return jax.shard_map(local, mesh=mesh, in_specs=(block, cells, cells, cells), out_specs=block, check_vma=False)
```
